256 devices in a mesh: enc: 4 (over y), seq: 16 (over z, core), mp: 4 (over x).
Axes of the slice: x: 4, y: 4, z: 8, core: 2. Of those that a mesh axis runs over, the one named last changes fastest.
Arguments:
- queries: bfloat16 [4, 2048, 4096], P('enc', 'seq', 'mp'), may hold values from -6 to 6
- keys_in: bfloat16 [4, 2048, 4096], P('enc', 'seq', 'mp'), may hold values from -6 to 6
- values_in: bfloat16 [4, 2048, 4096], P('enc', 'seq', 'mp'), may hold values from -6 to 6
- memory: bfloat16 [128, 128, 1024], P('enc', None, 'mp'), may hold values from -11 to 11
- enc_wq: bfloat16 [1024, 1024], P(None, 'mp'), may hold values from -1 to 1
- enc_wk: bfloat16 [1024, 1024], P(None, 'mp'), may hold values from -2 to 2
- enc_wv: bfloat16 [1024, 1024], P(None, 'mp'), may hold values from -0.1875 to 0.1875
- enc_wo: bfloat16 [1024, 1024], P('mp'), may hold values from -0.75 to 0.75
- cross_wk: bfloat16 [1024, 4096], P(None, 'mp'), may hold values from -0.1875 to 0.1875
- cross_wv: bfloat16 [1024, 4096], P(None, 'mp'), may hold values from -0.1875 to 0.1875
- cross_wq: bfloat16 [32, 128, 128], P('mp'), may hold values from -0.5 to 0.5
- nbr_rows: int32 [4, 32, 2], P('enc', 'seq'), may hold values from 0 to 31
- nbr_owner: int32 [4, 32, 2], P('enc', 'seq'), may hold values from 0 to 3, as said below
- nbr_count: int32 [4, 32], P('enc'), may hold values from 0 to 2, as said below
Outputs:
- attended: bfloat16 [4, 2048, 4096], P('enc', 'seq', 'mp')
The draws below stay inside these ranges and needn't reach their ends.
Inputs may be any that keep to these rules, and one draw needn't show every extreme that they name: `nbr_owner`: the 2 neighbours of a span have different owners; within the spans of one index of seq (aligned blocks of 2 spans of a sequence) no owner holds more than 2 neighbours, and some owner holds exactly 2 in every block. `nbr_count`: the spans of each sequence's first 128 tokens have 2 live neighbours.
All inputs are finite; a program needn't handle non-finite values.
Results may differ from the reference program's by a relative error of at most 0.029.
The reference program's roundings to bfloat16 on the way count: a program that leaves them out, or rounds other values in their place, can miss the bound.
Values may be sent and summed in bfloat16 or wider, within the bound.
No kernel may reach another device: no remote copies, remote signals or barrier semaphores. Data moves between devices by JAX's collectives and lax.ppermute only.
A program may use at most 128 MiB of HBM per device.

```python
import math
import jax
import jax.numpy as jnp
from jax import lax

DE = 1024
H = 32
HEAD_DIM = 128
NT = 128
SPAN = 64
K_NB = 2
TOK_DEV = 128
DB_DEV = 32
SEQS = 4
TOKENS = 2048
SPANS = 32


def block_order(block_key):
    return jax.random.permutation(block_key, SEQS)


def random_signs(key, shape):
    return (jax.random.randint(key, shape, 0, 2) * 2 - 1).astype(jnp.float32)


def plant_layout(key):
    layout_key = jax.random.fold_in(key, 501)
    sign_key, first_key, later_key = jax.random.split(layout_key, 3)
    signs = random_signs(sign_key, (SEQS, 3, H * HEAD_DIM))
    quarter = SPAN // 4
    key_rows = jnp.arange(3)[None, :] * quarter + jax.random.randint(first_key, (SEQS, 3), 0, quarter - 1)
    stride = (TOK_DEV - 1) // 3
    query_rows = SPAN + jnp.arange(3)[None, :] * stride + jax.random.randint(later_key, (SEQS, 3), 0, stride)
    return (signs, key_rows.astype(jnp.int32), query_rows.astype(jnp.int32))


def normal_rows(key, shape):
    return jnp.clip(jax.random.normal(key, shape, jnp.float32), -6.0, 6.0)


def plant(base, rows, planted):
    seq_ids = jnp.broadcast_to(jnp.arange(SEQS)[:, None], rows.shape)
    return base.at[seq_ids, rows].set(planted)


def shared_weight(key):
    return jnp.clip(jax.random.normal(jax.random.fold_in(key, 601), (DE, DE), jnp.float32), -6.0, 6.0)


def draw_queries(key, part):
    signs, key_rows, query_rows = plant_layout(key)
    key = jax.random.fold_in(key, 31)
    shape = (SEQS, TOKENS, H * HEAD_DIM)
    base = normal_rows(key, shape)
    strength = jnp.array([3.0, 4.5, 6.0], jnp.float32)
    return plant(base, query_rows, signs * strength[None, :, None]).astype(jnp.bfloat16)


def draw_keys_in(key, part):
    signs, key_rows, query_rows = plant_layout(key)
    key = jax.random.fold_in(key, 37)
    shape = (SEQS, TOKENS, H * HEAD_DIM)
    base = normal_rows(key, shape)
    base = plant(base, key_rows, 6.0 * signs)
    return plant(base, key_rows + 1, 5.96875 * signs).astype(jnp.bfloat16)


def draw_values_in(key, part):
    signs, key_rows, query_rows = plant_layout(key)
    key = jax.random.fold_in(key, 43)
    base_key, first_key, second_key = jax.random.split(key, 3)
    shape = (SEQS, TOKENS, H * HEAD_DIM)
    base = normal_rows(base_key, shape)
    base = plant(base, key_rows, 6.0 * random_signs(first_key, (SEQS, 3, H * HEAD_DIM)))
    return plant(base, key_rows + 1, 6.0 * random_signs(second_key, (SEQS, 3, H * HEAD_DIM))).astype(jnp.bfloat16)


def draw_memory(key, part):
    key = jax.random.fold_in(key, 47)
    shape = (SEQS * DB_DEV, NT, DE)
    base = normal_rows(key, shape)
    return base.astype(jnp.bfloat16)


def draw_enc_wq(key, part):
    common = shared_weight(key)
    return (common * DE ** (-0.5)).astype(jnp.bfloat16)


def draw_enc_wk(key, part):
    key = jax.random.fold_in(key, 59)
    fresh = normal_rows(key, (DE, DE))
    mixed = fresh
    return (mixed * DE ** (-0.5)).astype(jnp.bfloat16)


def draw_nbr_owner(key, part):
    key = jax.random.fold_in(key, 11)
    span_dev = TOK_DEV // SPAN
    blocks = SEQS * SPANS // span_dev
    block_keys = jax.random.split(key, blocks)
    orders = jax.vmap(block_order)(block_keys)
    span_ids = jnp.arange(span_dev)
    first_owner = orders[:, span_ids % SEQS]
    second_owner = orders[:, (span_ids + 1) % SEQS]
    flip_draw = jax.random.randint(jax.random.fold_in(key, 1), (blocks, span_dev), 0, 2)
    owner_left = jnp.where(flip_draw == 1, second_owner, first_owner)
    owner_right = jnp.where(flip_draw == 1, first_owner, second_owner)
    return jnp.stack([owner_left, owner_right], axis=-1).reshape(SEQS, SPANS, K_NB).astype(jnp.int32)


def draw_nbr_count(key, part):
    key = jax.random.fold_in(key, 23)
    drawn_counts = jnp.minimum(jax.random.randint(key, (SEQS, SPANS), 0, 4), K_NB)
    first_block = jnp.arange(SPANS)[None, :] < TOK_DEV // SPAN
    return jnp.where(first_block, K_NB, drawn_counts).astype(jnp.int32)


def place_ends(drawn, own_key, low, top_value):
    longest = drawn.shape.index(max(drawn.shape))
    spots = []
    for shift in (0, 1):
        where = [jax.random.randint(jax.random.fold_in(own_key, axis), (), 0, length) for axis, length in enumerate(drawn.shape)]
        where[longest] = (where[longest] + shift) % drawn.shape[longest]
        spots.append(tuple(where))
    return drawn.at[spots[0]].set(low).at[spots[1]].set(top_value)


def steps_of(own_key, dims, cuts, least, top_value):
    def one(dim, parts):
        draws = jax.random.uniform(jax.random.fold_in(jax.random.fold_in(own_key, 6), dim), (parts,), jnp.float32, least / len(cuts), top_value / len(cuts))
        return jnp.repeat(jnp.exp(draws), dims[dim] // parts).reshape((-1,) + (1,) * (len(dims) - dim - 1))

    gain = one(*cuts[0])
    for cut in cuts[1:]:
        gain = gain * one(*cut)
    return gain


def scatter_about(rng, shape, deviation, limit, cuts=(), held_as=jnp.bfloat16):
    drawn = jax.random.normal(rng, shape, jnp.float32) * deviation
    if len(cuts) > 0:
        drawn = steps_of(rng, shape, cuts, -0.22, 0.18) * drawn
    return jnp.clip(drawn, min=-limit, max=limit).astype(held_as)


def setup_inputs(seed: int = 0) -> dict:
    arg_keys = jax.random.split(jax.random.key(seed), 15)
    return {
        "queries": draw_queries(jax.random.fold_in(arg_keys[14], 71), 0),
        "keys_in": draw_keys_in(jax.random.fold_in(arg_keys[14], 71), 0),
        "values_in": draw_values_in(jax.random.fold_in(arg_keys[14], 71), 0),
        "memory": draw_memory(jax.random.fold_in(arg_keys[14], 71), 0),
        "enc_wq": draw_enc_wq(jax.random.fold_in(arg_keys[14], 71), 0),
        "enc_wk": draw_enc_wk(jax.random.fold_in(arg_keys[14], 71), 0),
        "enc_wv": scatter_about(arg_keys[6], (DE, DE), DE ** -0.5, 0.1875, ((1, 4),)),
        "enc_wo": scatter_about(arg_keys[7], (DE, DE), (DE // 16) ** -0.5, 0.75, ((0, 4),)),
        "cross_wk": scatter_about(arg_keys[8], (DE, H * HEAD_DIM), DE ** -0.5, 0.1875, ((1, 4),)),
        "cross_wv": scatter_about(arg_keys[9], (DE, H * HEAD_DIM), DE ** -0.5, 0.1875, ((1, 4),)),
        "cross_wq": scatter_about(arg_keys[10], (H, HEAD_DIM, HEAD_DIM), HEAD_DIM ** -0.5, 0.5, ((0, 4),)),
        "nbr_rows": place_ends(jax.random.randint(arg_keys[11], (SEQS, SPANS, K_NB), 0, DB_DEV), jax.random.fold_in(arg_keys[11], 1), 0, DB_DEV - 1).astype(jnp.int32),
        "nbr_owner": draw_nbr_owner(jax.random.fold_in(arg_keys[14], 71), 0),
        "nbr_count": draw_nbr_count(jax.random.fold_in(arg_keys[14], 71), 0),
    }


NEG_BIG = -1e+30

def masked_softmax(scores, alive_mask):
    masked = jnp.where(alive_mask, scores, NEG_BIG)
    highest = lax.optimization_barrier(jnp.max(masked, axis=-1, keepdims=True))
    weights = jnp.where(alive_mask, jnp.exp(masked - highest), 0.0)
    return (weights, lax.optimization_barrier(jnp.sum(weights, axis=-1, keepdims=True)))

def encode_one(source, enc_wq, enc_wk, enc_wv, enc_wo):
    enc_heads = DE // HEAD_DIM
    score_scale = 1.0 / math.sqrt(HEAD_DIM)

    def project(weight):
        return jnp.dot(source, weight, preferred_element_type=jnp.float32).astype(jnp.bfloat16).reshape(NT, enc_heads, HEAD_DIM)
    enc_query = project(enc_wq)
    enc_key = project(enc_wk)
    enc_value = project(enc_wv)
    scores = jnp.einsum('thd,uhd->htu', enc_query.astype(jnp.float32), enc_key.astype(jnp.float32)) * score_scale
    weights, totals = masked_softmax(scores, True)
    rounded = lax.optimization_barrier(weights.astype(jnp.bfloat16))
    enc_mix = jnp.einsum('htu,uhd->thd', rounded.astype(jnp.float32), enc_value.astype(jnp.float32)) / jnp.transpose(totals, (1, 0, 2))
    enc_attn = enc_mix.astype(jnp.bfloat16).reshape(NT, DE)
    return (source.astype(jnp.float32) + jnp.dot(enc_attn, enc_wo, preferred_element_type=jnp.float32)).astype(jnp.bfloat16)

def head_major(values):
    return jnp.transpose(values.reshape(TOKENS, H, HEAD_DIM), (1, 0, 2))

def reference(queries, keys_in, values_in, memory, enc_wq, enc_wk, enc_wv, enc_wo, cross_wk, cross_wv, cross_wq, nbr_rows, nbr_owner, nbr_count):
    score_scale = 1.0 / math.sqrt(HEAD_DIM)
    positions = jnp.arange(TOKENS)
    causal = positions[None, :] <= positions[:, None]

    def encode_row(row_index):
        source = lax.dynamic_index_in_dim(memory, row_index, 0, keepdims=False)
        return encode_one(source, enc_wq, enc_wk, enc_wv, enc_wo)

    def one_head(operands):
        head_q, head_k, head_v = operands
        scores = jnp.dot(head_q, head_k.T, preferred_element_type=jnp.float32) * score_scale
        weights, totals = masked_softmax(scores, causal)
        return (jnp.dot(weights.astype(jnp.bfloat16), head_v, preferred_element_type=jnp.float32) / totals).astype(jnp.bfloat16)

    def one_sequence(operands):
        seq_q, seq_k, seq_v, rows, owners, counts = operands
        flat_index = (owners * DB_DEV + rows).reshape(-1).astype(jnp.int32)
        encoded = lax.map(encode_row, flat_index)
        enc_flat = encoded.reshape(SPANS * K_NB * NT, DE)
        cross_k = jnp.dot(enc_flat, cross_wk, preferred_element_type=jnp.float32).astype(jnp.bfloat16).reshape(SPANS, K_NB * NT, H, HEAD_DIM)
        cross_v = jnp.dot(enc_flat, cross_wv, preferred_element_type=jnp.float32).astype(jnp.bfloat16).reshape(SPANS, K_NB * NT, H, HEAD_DIM)
        self_out = jnp.transpose(lax.map(one_head, (head_major(seq_q), head_major(seq_k), head_major(seq_v))), (1, 0, 2))
        cross_query = jnp.einsum('thd,hde->the', self_out.astype(jnp.float32), cross_wq.astype(jnp.float32)).astype(jnp.bfloat16)
        padded = jnp.concatenate([jnp.zeros((1, H, HEAD_DIM), jnp.bfloat16), cross_query, jnp.zeros((SPAN - 1, H, HEAD_DIM), jnp.bfloat16)], axis=0)
        padded = padded.reshape(SPANS + 1, SPAN, H, HEAD_DIM)
        ext_k = jnp.concatenate([jnp.zeros((1, K_NB * NT, H, HEAD_DIM), jnp.bfloat16), cross_k], axis=0)
        ext_v = jnp.concatenate([jnp.zeros((1, K_NB * NT, H, HEAD_DIM), jnp.bfloat16), cross_v], axis=0)
        ext_counts = jnp.concatenate([jnp.zeros((1,), jnp.int32), counts.astype(jnp.int32)])
        alive_mask = (jnp.arange(K_NB * NT) // NT)[None, :] < ext_counts[:, None]
        scores = jnp.einsum('ethd,ekhd->ehtk', padded.astype(jnp.float32), ext_k.astype(jnp.float32)) * score_scale
        weights, totals = masked_softmax(scores, alive_mask[:, None, None, :])
        rounded = lax.optimization_barrier(weights.astype(jnp.bfloat16))
        cross_mix = jnp.einsum('ehtk,ekhd->ethd', rounded.astype(jnp.float32), ext_v.astype(jnp.float32))
        cross_mix = cross_mix / jnp.maximum(jnp.transpose(totals, (0, 2, 1, 3)), 1.0)
        cross_out = cross_mix.reshape((SPANS + 1) * SPAN, H, HEAD_DIM)[1:TOKENS + 1]
        return (self_out.astype(jnp.float32) + cross_out).astype(jnp.bfloat16).reshape(TOKENS, H * HEAD_DIM)
    return lax.map(one_sequence, (queries, keys_in, values_in, nbr_rows, nbr_owner, nbr_count))
```

```python
import math

import jax
import jax.numpy as jnp
from jax import lax
from jax.experimental import pallas as pl
from jax.experimental.pallas import tpu as pltpu
from jax.sharding import PartitionSpec as P

HEAD_DIM = 128
SPAN = 64
K_NB = 2
NT = 128
DB = 32
N_ENC = 4
N_MP = 4
N_Z = 8
NEG_BIG = -1e30
SCALE = 1.0 / math.sqrt(HEAD_DIM)
EXP2_SCALE = SCALE * math.log2(math.e)
BF = jnp.bfloat16
F32 = jnp.float32

ANY = pl.BlockSpec(memory_space=pl.ANY)
SMEM = pl.BlockSpec(memory_space=pltpu.SMEM)
VMEM = pl.BlockSpec(memory_space=pltpu.VMEM)
MB = 1024 * 1024


def shifted(block, axis, distance):
    size = lax.axis_size(axis)
    return lax.ppermute(block, axis, [(i, (i + distance) % size) for i in range(size)])


def core_swap(block):
    size = lax.axis_size("seq")
    return lax.ppermute(block, "seq", [(i, i ^ 1) for i in range(size)])


def sds(shape, dtype=BF):
    return jax.ShapeDtypeStruct(shape, dtype)


def params(limit_mb):
    return pltpu.CompilerParams(vmem_limit_bytes=limit_mb * MB)


def cost(flops, nbytes, trans=0):
    return pl.CostEstimate(flops=flops, bytes_accessed=nbytes, transcendentals=trans)


def dot(a, b):
    return jnp.dot(a, b, preferred_element_type=F32)


def dot_t(a, b):
    return lax.dot_general(a, b, (((1,), (1,)), ((), ())), preferred_element_type=F32)


def run_copies(pairs, sems):
    copies = [pltpu.make_async_copy(s, d, sems.at[n]) for n, (s, d) in enumerate(pairs)]
    for c in copies:
        c.start()
    return copies


def fetch_kernel(idx0, idx1, idx2, idx3, memory, s0, s1, s2, s3, sems):
    me = lax.axis_index("enc")
    pairs = []
    for idx, out in ((idx0, s0), (idx1, s1), (idx2, s2), (idx3, s3)):
        for span in range(2):
            row = jnp.int32(0)
            for j in range(K_NB):
                flat = idx[span * K_NB + j]
                row = jnp.where(flat // DB == me, flat % DB, row)
            pairs.append((memory.at[row], out.at[pl.ds(span * NT, NT)]))
    for c in run_copies(pairs, sems):
        c.wait()


def fetch(idx, memory):
    cols = memory.shape[2]
    return pl.pallas_call(
        fetch_kernel,
        out_shape=[sds((2 * NT, cols))] * 4,
        in_specs=[SMEM] * 4 + [ANY],
        out_specs=[ANY] * 4,
        scratch_shapes=[pltpu.SemaphoreType.DMA((8,))],
        compiler_params=params(4),
        cost_estimate=cost(0, 1 * MB),
        name="fetch",
    )(*idx, memory)


def compact_kernel(idx, r0, r1, r2, r3, out_a, out_b, sems):
    me = lax.axis_index("enc")

    def each(act):
        for span, out in enumerate((out_a, out_b)):
            for j in range(K_NB):
                at = (idx[span * K_NB + j] // DB - me + N_ENC) % N_ENC
                for k, r in enumerate((r0, r1, r2, r3)):

                    @pl.when(at == k)
                    def _():
                        act(
                            pltpu.make_async_copy(
                                r.at[pl.ds(span * NT, NT)],
                                out.at[pl.ds(j * NT, NT)],
                                sems.at[span * K_NB + j],
                            )
                        )

    each(lambda c: c.start())
    each(lambda c: c.wait())


def compact(idx, received):
    shape = received[0].shape
    return pl.pallas_call(
        compact_kernel,
        out_shape=[sds(shape)] * 2,
        in_specs=[SMEM] + [ANY] * 4,
        out_specs=[ANY] * 2,
        scratch_shapes=[pltpu.SemaphoreType.DMA((4,))],
        compiler_params=params(4),
        cost_estimate=cost(0, MB // 2),
        name="compact",
    )(idx, *received)


def source_columns(k, width):
    col = (lax.axis_index("mp") - k + N_MP) % N_MP
    return pl.ds(pl.multiple_of(col * width, width), width)


def encode_kernel(x0, x1, x2, x3, wq, wk, wv, out, src, wq_s, wk_s, wv_s, sems):
    width = x0.shape[1]
    pairs = [(x, src.at[:, source_columns(k, width)]) for k, x in enumerate((x0, x1, x2, x3))]
    pairs += [(wq, wq_s), (wk, wk_s), (wv, wv_s)]
    for c in run_copies(pairs, sems):
        c.wait()
    source = src[...]
    q = dot(source, wq_s[...]).astype(BF)
    k = dot(source, wk_s[...]).astype(BF)
    v = dot(source, wv_s[...]).astype(BF)
    for n in range(src.shape[0] // NT):
        rows = slice(n * NT, (n + 1) * NT)
        for h in range(width // HEAD_DIM):
            cols = slice(h * HEAD_DIM, (h + 1) * HEAD_DIM)
            s = dot_t(q[rows, cols], k[rows, cols])
            p = jnp.exp2((s - jnp.max(s, axis=-1, keepdims=True)) * EXP2_SCALE)
            total = jnp.sum(p, axis=-1, keepdims=True)
            out[rows, cols] = (dot(p.astype(BF), v[rows, cols]) / total).astype(BF)


def encode(pieces, wq, wk, wv):
    rows, width = pieces[0].shape
    depth = wq.shape[0]
    weight = pltpu.VMEM((depth, width), BF)
    return pl.pallas_call(
        encode_kernel,
        out_shape=sds((rows, width)),
        in_specs=[ANY] * 7,
        out_specs=VMEM,
        scratch_shapes=[pltpu.VMEM((rows, depth), BF), weight, weight, weight, pltpu.SemaphoreType.DMA((7,))],
        compiler_params=params(16),
        cost_estimate=cost(2 * rows * depth * width * 3, 3 * MB),
        name="encode",
    )(*pieces, wq, wk, wv)


def cross_kernel(
    row_begin, which, counts,
    x0, x1, x2, x3, a0, a1, a2, a3, wo, wk, wv, cq, so,
    out, src, attn, wo_s, wk_s, wv_s, cq_s, so_s, sems,
):
    width = x0.shape[1]
    pairs = [(a, attn.at[:, pl.ds(k * width, width)]) for k, a in enumerate((a0, a1, a2, a3))]
    pairs += [(x, src.at[:, source_columns(k, width)]) for k, x in enumerate((x0, x1, x2, x3))]
    rows = pl.ds(row_begin, SPAN)
    pairs += [(cq.at[rows], cq_s), (so.at[rows], so_s), (wo, wo_s), (wk, wk_s), (wv, wv_s)]
    copies = run_copies(pairs, sems)
    for c in copies[:11]:
        c.wait()
    seq = lax.axis_index("seq")
    count = counts[0, seq * 2 + which]
    encoded = (src[...].astype(F32) + dot(attn[...], wo_s[...])).astype(BF)
    copies[11].wait()
    keys = dot(encoded, wk_s[...]).astype(BF)
    copies[12].wait()
    values = dot(encoded, wv_s[...]).astype(BF)
    shape = (SPAN, K_NB * NT)
    alive = lax.broadcasted_iota(jnp.int32, shape, 1) < count * NT
    if which == 1:
        past = (lax.broadcasted_iota(jnp.int32, shape, 0) > 0) & (seq == lax.axis_size("seq") - 1)
        alive = alive & jnp.logical_not(past)
    for h in range(cq_s.shape[1] // HEAD_DIM):
        cols = slice(h * HEAD_DIM, (h + 1) * HEAD_DIM)
        s = dot_t(cq_s[:, cols], keys[:, cols])
        s = jnp.where(alive, s, NEG_BIG)
        p = jnp.exp2((s - jnp.max(s, axis=-1, keepdims=True)) * EXP2_SCALE)
        p = jnp.where(alive, p, 0.0)
        total = jnp.maximum(jnp.sum(p, axis=-1, keepdims=True), 1.0)
        mix = dot(p.astype(BF), values[:, cols]) / total
        out[:, cols] = (so_s[:, cols].astype(F32) + mix).astype(BF)


def cross(which, counts, pieces, attn, wo, wk, wv, cq, so):
    rows, width = pieces[0].shape
    depth, cols = wk.shape
    row_begin = which * SPAN

    def body(*refs):
        cross_kernel(row_begin, which, *refs)

    span_rows = pltpu.VMEM((SPAN, cols), BF)
    return pl.pallas_call(
        body,
        out_shape=sds((SPAN, cols)),
        in_specs=[SMEM] + [ANY] * 13,
        out_specs=VMEM,
        scratch_shapes=[
            pltpu.VMEM((rows, depth), BF),
            pltpu.VMEM((rows, depth), BF),
            pltpu.VMEM((depth, depth), BF),
            pltpu.VMEM((depth, cols), BF),
            pltpu.VMEM((depth, cols), BF),
            span_rows,
            span_rows,
            pltpu.SemaphoreType.DMA((13,)),
        ],
        compiler_params=params(24),
        cost_estimate=cost(2 * rows * depth * cols * 3, 8 * MB),
        name="cross",
    )(counts, *pieces, *attn, wo, wk, wv, cq, so)


def pack_kernel(q, k, v, *refs):
    outs, sems = refs[:N_Z], refs[N_Z]
    z = lax.axis_index("seq") // 2
    tok = q.shape[1]
    pairs = []
    for d, out in enumerate(outs):
        head = (z + d) % N_Z
        cols = pl.ds(pl.multiple_of(head * HEAD_DIM, HEAD_DIM), HEAD_DIM)
        for n, ref in enumerate((q, k, v)):
            pairs.append((ref.at[0, :, cols], out.at[pl.ds(n * tok, tok)]))
    for c in run_copies(pairs, sems):
        c.wait()


def pack(q, k, v):
    tok = q.shape[1]
    return pl.pallas_call(
        pack_kernel,
        out_shape=[sds((3 * tok, HEAD_DIM))] * N_Z,
        in_specs=[ANY] * 3,
        out_specs=[ANY] * N_Z,
        scratch_shapes=[pltpu.SemaphoreType.DMA((3 * N_Z,))],
        compiler_params=params(4),
        cost_estimate=cost(0, 2 * MB),
        name="pack",
    )(q, k, v)


def collect_kernel(*refs):
    ins, q_out, swap_out, sems = refs[:N_Z], refs[N_Z], refs[N_Z + 1], refs[N_Z + 2]
    z = lax.axis_index("seq") // 2
    tok = ins[0].shape[0] // 3
    total = N_Z * tok
    pairs = []
    for d, ref in enumerate(ins):
        at = (z - d + N_Z) % N_Z
        rows = pl.ds(pl.multiple_of(at * tok, tok), tok)
        half = tok // 2
        pairs.append((ref.at[pl.ds(0, tok)], q_out.at[rows]))
        pairs.append((ref.at[pl.ds(tok, tok)], swap_out.at[rows]))
        rows = pl.ds(pl.multiple_of(at * tok + total, tok), tok)
        pairs.append((ref.at[pl.ds(2 * tok, tok)], swap_out.at[rows]))
        rows = pl.ds(pl.multiple_of(at * half + 2 * total, half), half)
        pairs.append((ref.at[pl.ds(0, half)], swap_out.at[rows]))
    for c in run_copies(pairs, sems):
        c.wait()


def collect(pieces):
    tok = pieces[0].shape[0] // 3
    total = N_Z * tok
    return pl.pallas_call(
        collect_kernel,
        out_shape=[sds((total, HEAD_DIM)), sds((2 * total + total // 2, HEAD_DIM))],
        in_specs=[ANY] * N_Z,
        out_specs=[ANY] * 2,
        scratch_shapes=[pltpu.SemaphoreType.DMA((4 * N_Z,))],
        compiler_params=params(4),
        cost_estimate=cost(0, 2 * MB),
        name="collect",
    )(*pieces)


def attend_kernel(q, own, other, *refs):
    outs, acc = refs[:N_Z], refs[N_Z]
    z_me = lax.axis_index("seq") // 2
    core = lax.axis_index("seq") % 2
    total = q.shape[0]
    tok = total // N_Z
    half = tok // 2
    tokens = 2 * total
    for z in range(N_Z):
        mine = q[z * tok : (z + 1) * tok, :]
        base = 2 * total
        next0 = other[base + z * half : base + (z + 1) * half, :]
        after = (z + 1) % N_Z
        next1 = other[base + after * half : base + (after + 1) * half, :]
        nxt = jnp.where(core == 0, next0.astype(F32), next1.astype(F32))
        both = jnp.concatenate([mine.astype(F32), nxt], axis=0)
        rolled = pltpu.roll(both, both.shape[0] - (SPAN - 1), 0)[:tok].astype(BF)
        block = 2 * z + core
        pos = block * tok + SPAN - 1 + lax.broadcasted_iota(jnp.int32, (tok, 1), 0)
        pos = jnp.where(pos >= tokens, pos - tokens, pos)
        n_own, n_other = z + 1, min(z + 2, N_Z)
        s_own = dot_t(rolled, own[: n_own * tok, :])
        s_other = dot_t(rolled, other[: n_other * tok, :])
        col = lax.broadcasted_iota(jnp.int32, (1, tok), 1)
        parts = []
        for n, s, parity in ((n_own, s_own, core), (n_other, s_other, 1 - core)):
            for b in range(n):
                piece = s[:, b * tok : (b + 1) * tok]
                if b >= z or z == N_Z - 1:
                    piece = jnp.where((2 * b + parity) * tok + col <= pos, piece, NEG_BIG)
                parts.append(piece)
        s = jnp.concatenate(parts, axis=1)
        p = jnp.exp2((s - jnp.max(s, axis=-1, keepdims=True)) * EXP2_SCALE)
        norm = jnp.sum(p, axis=-1, keepdims=True)
        p = p.astype(BF)
        mix = dot(p[:, : n_own * tok], own[total : total + n_own * tok, :])
        mix = mix + dot(p[:, n_own * tok :], other[total : total + n_other * tok, :])
        acc[z * tok : (z + 1) * tok, :] = (mix / norm).astype(BF)
    for d, out in enumerate(outs):
        rows = pl.ds(pl.multiple_of(((z_me + d) % N_Z) * tok, tok), tok)
        out[...] = acc[rows, :]


def attend(q, own, other):
    total = q.shape[0]
    tok = total // N_Z
    return pl.pallas_call(
        attend_kernel,
        out_shape=[sds((tok, HEAD_DIM))] * N_Z,
        in_specs=[VMEM] * 3,
        out_specs=[VMEM] * N_Z,
        scratch_shapes=[pltpu.VMEM((total, HEAD_DIM), BF)],
        compiler_params=params(24),
        cost_estimate=cost(2 * 2 * total * total * HEAD_DIM, 2 * MB, total * total),
        name="attend",
    )(q, own, other)


def query_kernel(*refs):
    ins, wq, so, cq = refs[:N_Z], refs[N_Z], refs[N_Z + 1], refs[N_Z + 2]
    z = lax.axis_index("seq") // 2
    for d, ref in enumerate(ins):
        head = (z - d + N_Z) % N_Z
        cols = pl.ds(pl.multiple_of(head * HEAD_DIM, HEAD_DIM), HEAD_DIM)
        value = ref[...]
        so[:, cols] = value
        cq[:, cols] = dot(value, wq[head]).astype(BF)


def cross_queries(pieces, wq):
    tok = pieces[0].shape[0]
    cols = N_Z * HEAD_DIM
    return pl.pallas_call(
        query_kernel,
        out_shape=[sds((tok, cols))] * 2,
        in_specs=[VMEM] * (N_Z + 1),
        out_specs=[VMEM] * 2,
        compiler_params=params(8),
        cost_estimate=cost(2 * tok * cols * HEAD_DIM, MB),
        name="cross_queries",
    )(*pieces, wq)


def whole_wo_kernel(own, h1, h2, h3, swapped, out, sems):
    half = h1.shape[0]
    core = lax.axis_index("seq") % 2
    pairs = [(own, out.at[pl.ds(0, 2 * half)])]
    for k, ref in enumerate((h1, h2, h3)):
        base = (k + 1) * 2 * half
        rows = pl.ds(pl.multiple_of(base + core * half, half), half)
        pairs.append((ref, out.at[rows]))
        rows = pl.ds(pl.multiple_of(base + (1 - core) * half, half), half)
        pairs.append((swapped.at[pl.ds(k * half, half)], out.at[rows]))
    for c in run_copies(pairs, sems):
        c.wait()


def gathered_wo(wo):
    rows, cols = wo.shape
    half = rows // 2
    core = lax.axis_index("seq") % 2
    mine = lax.dynamic_slice_in_dim(wo, core * half, half, 0)
    got = [shifted(mine, "mp", k) for k in range(1, N_MP)]
    swapped = core_swap(jnp.concatenate(got, axis=0))
    return pl.pallas_call(
        whole_wo_kernel,
        out_shape=sds((N_MP * rows, cols)),
        in_specs=[ANY] * 5,
        out_specs=ANY,
        scratch_shapes=[pltpu.SemaphoreType.DMA((7,))],
        compiler_params=params(4),
        cost_estimate=cost(0, 4 * MB),
        name="whole_wo",
    )(wo, *got, swapped)


def place_kernel(received, first, second, out):
    rows = jnp.concatenate([received[...], first[...], second[...]], axis=0).astype(F32)
    out[0] = pltpu.roll(rows, rows.shape[0] - 1, 0)[: out.shape[1]].astype(BF)


def place(received, first, second):
    cols = first.shape[1]
    return pl.pallas_call(
        place_kernel,
        out_shape=sds((1, 2 * SPAN, cols)),
        in_specs=[VMEM] * 3,
        out_specs=VMEM,
        compiler_params=params(8),
        cost_estimate=cost(0, MB),
        name="place",
    )(received, first, second)


def per_device(
    queries, keys_in, values_in, memory, enc_wq, enc_wk, enc_wv, enc_wo,
    cross_wk, cross_wv, cross_wq, nbr_rows, nbr_owner, nbr_count,
):
    idx = (nbr_owner * DB + nbr_rows).reshape(-1)
    asked = [idx] + [shifted(idx, "enc", k) for k in range(1, N_ENC)]
    packed = pack(queries, keys_in, values_in)
    head_pieces = [packed[0]] + [shifted(packed[d], "seq", 2 * d) for d in range(1, N_Z)]
    wo = gathered_wo(enc_wo)

    sent = fetch(asked, memory)
    received = [sent[0]] + [shifted(sent[k], "enc", -k) for k in range(1, N_ENC)]
    mine = compact(idx, received)
    pieces = [[block] + [shifted(block, "mp", k) for k in range(1, N_MP)] for block in mine]

    q_all, own = collect(head_pieces)
    other = core_swap(own)
    back = attend(q_all, own, other)
    back = [back[0]] + [shifted(back[d], "seq", 2 * d) for d in range(1, N_Z)]
    so, cq = cross_queries(back, cross_wq)

    attn = []
    for block in (1, 0):
        value = encode(pieces[block], enc_wq, enc_wk, enc_wv)
        attn.append([value] + [shifted(value, "mp", k) for k in range(1, N_MP)])
    second = cross(1, nbr_count, pieces[1], attn[0], wo, cross_wk, cross_wv, cq, so)
    passed = shifted(second, "seq", 1)
    first = cross(0, nbr_count, pieces[0], attn[1], wo, cross_wk, cross_wv, cq, so)
    return place(passed, first, second)


def solution(mesh):
    return jax.shard_map(
        per_device,
        mesh=mesh,
        in_specs=(
            P("enc", "seq", "mp"),
            P("enc", "seq", "mp"),
            P("enc", "seq", "mp"),
            P("enc", None, "mp"),
            P(None, "mp"),
            P(None, "mp"),
            P(None, "mp"),
            P("mp", None),
            P(None, "mp"),
            P(None, "mp"),
            P("mp", None, None),
            P("enc", "seq", None),
            P("enc", "seq", None),
            P("enc", None),
        ),
        out_specs=P("enc", "seq", "mp"),
        check_vma=False,
    )
```

```python
import math

import jax
import jax.numpy as jnp
from jax import lax
from jax.experimental import pallas as pl
from jax.experimental.pallas import tpu as pltpu
from jax.sharding import PartitionSpec as P

HEAD_DIM = 128
SPAN = 64
K_NB = 2
NT = 128
DB = 32
N_ENC = 4
N_MP = 4
N_Z = 8
NEG_BIG = -1e30
SCALE = 1.0 / math.sqrt(HEAD_DIM)
EXP2_SCALE = SCALE * math.log2(math.e)
BF = jnp.bfloat16
F32 = jnp.float32

ANY = pl.BlockSpec(memory_space=pl.ANY)
SMEM = pl.BlockSpec(memory_space=pltpu.SMEM)
VMEM = pl.BlockSpec(memory_space=pltpu.VMEM)
MB = 1024 * 1024


def shifted(block, axis, distance):
    size = lax.axis_size(axis)
    return lax.ppermute(block, axis, [(i, (i + distance) % size) for i in range(size)])


def to_sides(block):
    seqs, mps = lax.axis_size("seq"), lax.axis_size("mp")
    route = [
        (s * mps + m, s * mps + (m + (1 if s % 2 == 0 else -1)) % mps)
        for s in range(seqs)
        for m in range(mps)
    ]
    return lax.ppermute(block, ("seq", "mp"), route)


def core_swap(block):
    size = lax.axis_size("seq")
    return lax.ppermute(block, "seq", [(i, i ^ 1) for i in range(size)])


def over_z(blocks):
    groups = [[2 * z + core for z in range(N_Z)] for core in range(2)]
    return lax.all_to_all(blocks, "seq", 0, 0, axis_index_groups=groups, tiled=True)


def in_hbm(x):
    return pltpu.with_memory_space_constraint(x, pltpu.HBM)


def after(x, *others):
    def kernel(*refs):
        pass

    return pl.pallas_call(
        kernel,
        out_shape=sds(x.shape, x.dtype),
        in_specs=[ANY] * (1 + len(others)),
        out_specs=ANY,
        input_output_aliases={0: 0},
        compiler_params=params(1),
        cost_estimate=cost(0, 1024),
        name="after",
    )(x, *others)


def sds(shape, dtype=BF):
    return jax.ShapeDtypeStruct(shape, dtype)


def params(limit_mb):
    return pltpu.CompilerParams(vmem_limit_bytes=limit_mb * MB)


def cost(flops, nbytes, trans=0):
    return pl.CostEstimate(flops=flops, bytes_accessed=nbytes, transcendentals=trans)


def dot(a, b):
    return jnp.dot(a, b, preferred_element_type=F32)


def dot_t(a, b):
    return lax.dot_general(a, b, (((1,), (1,)), ((), ())), preferred_element_type=F32)


def run_copies(pairs, sems):
    copies = [pltpu.make_async_copy(s, d, sems.at[n]) for n, (s, d) in enumerate(pairs)]
    for c in copies:
        c.start()
    return copies


def fetch_kernel(idx0, idx1, idx2, idx3, memory, s0, s1, s2, s3, sems):
    me = lax.axis_index("enc")
    pairs = []
    for idx, out in ((idx0, s0), (idx1, s1), (idx2, s2), (idx3, s3)):
        for span in range(2):
            row = jnp.int32(0)
            for j in range(K_NB):
                flat = idx[span * K_NB + j]
                row = jnp.where(flat // DB == me, flat % DB, row)
            pairs.append((memory.at[row], out.at[pl.ds(span * NT, NT)]))
    for c in run_copies(pairs, sems):
        c.wait()


def fetch(idx, memory):
    cols = memory.shape[2]
    return pl.pallas_call(
        fetch_kernel,
        out_shape=[sds((2 * NT, cols))] * 4,
        in_specs=[SMEM] * 4 + [ANY],
        out_specs=[ANY] * 4,
        scratch_shapes=[pltpu.SemaphoreType.DMA((8,))],
        compiler_params=params(1),
        cost_estimate=cost(20 * 10**9, 1024),
        name="fetch",
    )(*idx, in_hbm(memory))


def compact_kernel(idx, r0, r1, r2, r3, w1, w2, out, sems):
    me = lax.axis_index("enc")

    def each(act):
        for span in range(2):
            for j in range(K_NB):
                at = (idx[span * K_NB + j] // DB - me + N_ENC) % N_ENC
                for k, r in enumerate((r0, r1, r2, r3)):

                    @pl.when(at == k)
                    def _():
                        act(
                            pltpu.make_async_copy(
                                r.at[pl.ds(span * NT, NT)],
                                out.at[pl.ds((span * K_NB + j) * NT, NT)],
                                sems.at[span * K_NB + j],
                            )
                        )

    each(lambda c: c.start())
    each(lambda c: c.wait())


def compact(idx, received, others):
    rows, cols = received[0].shape
    return pl.pallas_call(
        compact_kernel,
        out_shape=pltpu.HBM((K_NB * rows, cols), BF),
        in_specs=[SMEM] + [ANY] * 6,
        out_specs=ANY,
        scratch_shapes=[pltpu.SemaphoreType.DMA((4,))],
        compiler_params=params(1),
        cost_estimate=cost(1 * 10**9, 1024),
        name="compact",
    )(idx, *received, *others)


def source_columns(k, width):
    col = (lax.axis_index("mp") - k + N_MP) % N_MP
    return pl.ds(pl.multiple_of(col * width, width), width)


def encode_kernel(x0, x1, x2, x3, wq, wk, wv, second, first, src_out, src, w, sems):
    width = x0.shape[1]
    pairs = [(x, src.at[:, source_columns(k, width)]) for k, x in enumerate((x0, x1, x2, x3))]
    pairs += [(ref, w.at[n]) for n, ref in enumerate((wq, wk, wv))]
    copies = run_copies(pairs, sems)
    for c in copies[:5]:
        c.wait()
    kept = pltpu.make_async_copy(src, src_out, sems.at[0])
    kept.start()
    source = src[...]
    q = dot(source, w[0]).astype(BF)
    copies[5].wait()
    k = dot(source, w[1]).astype(BF)
    copies[6].wait()
    v = dot(source, w[2]).astype(BF)
    for n in range(src.shape[0] // NT):
        rows = slice(n * NT, (n + 1) * NT)
        out = (first, second)[n // K_NB]
        out_rows = slice(n % K_NB * NT, (n % K_NB + 1) * NT)
        for h in range(width // HEAD_DIM):
            cols = slice(h * HEAD_DIM, (h + 1) * HEAD_DIM)
            s = dot_t(q[rows, cols], k[rows, cols])
            p = jnp.exp2((s - jnp.max(s, axis=-1, keepdims=True)) * EXP2_SCALE)
            total = jnp.sum(p, axis=-1, keepdims=True)
            out[out_rows, cols] = (dot(p.astype(BF), v[rows, cols]) / total).astype(BF)
    kept.wait()


def encode(pieces, wq, wk, wv):
    rows, width = pieces[0].shape
    depth = wq.shape[0]
    return pl.pallas_call(
        encode_kernel,
        out_shape=[sds((rows // 2, width))] * 2 + [pltpu.HBM((rows, depth), BF)],
        in_specs=[ANY] * 7,
        out_specs=[VMEM, VMEM, ANY],
        scratch_shapes=[
            pltpu.VMEM((rows, depth), BF),
            pltpu.VMEM((3, depth, width), BF),
            pltpu.SemaphoreType.DMA((7,)),
        ],
        compiler_params=params(12),
        cost_estimate=cost(30 * 10**9, 1024),
        name="encode",
    )(*pieces, *map(in_hbm, (wq, wk, wv)))


def load_kernel(w0, w_near, w2, w_swapped, wk, wv, tie, wo_out, wk_out, wv_out, sems):
    width = w0.shape[0]
    near = 1 + 2 * (lax.axis_index("seq") % 2)
    pairs = []
    for k, w in ((0, w0), (near, w_near), (2, w2), (4 - near, w_swapped)):
        pairs.append((w, wo_out.at[pl.ds(pl.multiple_of(k * width, width), width)]))
    for c in run_copies(pairs + [(wk, wk_out), (wv, wv_out)], sems):
        c.wait()


def load(wo, wk, wv, tie):
    depth, cols = wk.shape
    return pl.pallas_call(
        load_kernel,
        out_shape=[pltpu.VMEM((depth, depth), BF), pltpu.VMEM((depth, cols), BF), pltpu.VMEM((depth, cols), BF)],
        in_specs=[ANY] * 7,
        out_specs=[ANY] * 3,
        scratch_shapes=[pltpu.SemaphoreType.DMA((6,))],
        compiler_params=params(1),
        cost_estimate=cost(3 * 10**9, 1024),
        name="load",
    )(*map(in_hbm, (*wo, wk, wv)), tie)


def cross_kernel(
    which, counts, src, a0, a1, a2, a3, wo, wk, wv, cq, so,
    out, src_s, attn, sems,
):
    nbrs, width = a0.shape
    pairs = [(src.at[pl.ds(which * nbrs, nbrs)], src_s)]
    pairs += [(a, attn.at[:, pl.ds(k * width, width)]) for k, a in enumerate((a0, a1, a2, a3))]
    copies = run_copies(pairs, sems)
    seq = lax.axis_index("seq")
    count = counts[0, seq * 2 + which]
    shape = (SPAN, nbrs)
    alive = lax.broadcasted_iota(jnp.int32, shape, 1) < count * NT
    if which == 1:
        past = (lax.broadcasted_iota(jnp.int32, shape, 0) > 0) & (seq == lax.axis_size("seq") - 1)
        alive = alive & jnp.logical_not(past)
    for c in copies:
        c.wait()
    encoded = (src_s[...].astype(F32) + dot(attn[...], wo[...])).astype(BF)
    keys = dot(encoded, wk[...]).astype(BF)
    values = dot(encoded, wv[...]).astype(BF)
    rows = slice(which * SPAN, (which + 1) * SPAN)
    for h in range(cq.shape[1] // HEAD_DIM):
        cols = slice(h * HEAD_DIM, (h + 1) * HEAD_DIM)
        s = dot_t(cq[rows, cols], keys[:, cols])
        s = jnp.where(alive, s, NEG_BIG)
        p = jnp.exp2((s - jnp.max(s, axis=-1, keepdims=True)) * EXP2_SCALE)
        p = jnp.where(alive, p, 0.0)
        total = jnp.maximum(jnp.sum(p, axis=-1, keepdims=True), 1.0)
        mix = dot(p.astype(BF), values[:, cols]) / total
        out[:, cols] = (so[rows, cols].astype(F32) + mix).astype(BF)


def cross(which, counts, source, attn, wo, wk, wv, cq, so):
    rows, depth = source.shape
    cols = cq.shape[1]

    def body(*refs):
        cross_kernel(which, *refs)

    return pl.pallas_call(
        body,
        out_shape=sds((SPAN, cols)),
        in_specs=[SMEM] + [ANY] * 5 + [VMEM] * 5,
        out_specs=VMEM,
        scratch_shapes=[
            pltpu.VMEM((rows // 2, depth), BF),
            pltpu.VMEM((rows // 2, depth), BF),
            pltpu.SemaphoreType.DMA((5,)),
        ],
        compiler_params=params(12),
        cost_estimate=cost(5 * 10**9, 1024),
        name="cross",
    )(counts, in_hbm(source), *attn, wo, wk, wv, cq, so)


def pack_kernel(q, k, v, out, rows, sems):
    tok = q.shape[1]
    copies = run_copies([(ref.at[0], rows.at[n]) for n, ref in enumerate((q, k, v))], sems)
    for n, c in enumerate(copies):
        c.wait()
        for head in range(N_Z):
            cols = slice(head * HEAD_DIM, (head + 1) * HEAD_DIM)
            out[head, n * tok : (n + 1) * tok, :] = rows[n, :, cols]


def pack(q, k, v):
    _, tok, cols = q.shape
    return pl.pallas_call(
        pack_kernel,
        out_shape=sds((N_Z, 3 * tok, HEAD_DIM)),
        in_specs=[ANY] * 3,
        out_specs=VMEM,
        scratch_shapes=[pltpu.VMEM((3, tok, cols), BF), pltpu.SemaphoreType.DMA((3,))],
        compiler_params=params(4),
        cost_estimate=cost(1 * 10**9, 1024),
        name="pack",
    )(in_hbm(q), in_hbm(k), in_hbm(v))


def attend_kernel(own, other, out):
    core = lax.axis_index("seq") % 2
    tok = out.shape[1]
    tokens = 2 * N_Z * tok
    for z in range(N_Z):
        after = (z + 1) % N_Z
        nxt = jnp.where(core == 0, other[z, :SPAN].astype(F32), other[after, :SPAN].astype(F32))
        both = jnp.concatenate([own[z, :tok].astype(F32), nxt], axis=0)
        rolled = pltpu.roll(both, both.shape[0] - (SPAN - 1), 0)[:tok].astype(BF)
        block = 2 * z + core
        pos = block * tok + SPAN - 1 + lax.broadcasted_iota(jnp.int32, (tok, 1), 0)
        pos = jnp.where(pos >= tokens, pos - tokens, pos)
        col = lax.broadcasted_iota(jnp.int32, (1, tok), 1)
        parts, values = [], []
        for n, ref, parity in ((z + 1, own, core), (min(z + 2, N_Z), other, 1 - core)):
            s = dot_t(rolled, ref[:n, tok : 2 * tok].reshape(n * tok, HEAD_DIM))
            values.append(ref[:n, 2 * tok :].reshape(n * tok, HEAD_DIM))
            for b in range(n):
                piece = s[:, b * tok : (b + 1) * tok]
                if b >= z or z == N_Z - 1:
                    piece = jnp.where((2 * b + parity) * tok + col <= pos, piece, NEG_BIG)
                parts.append(piece)
        s = jnp.concatenate(parts, axis=1)
        p = jnp.exp2((s - jnp.max(s, axis=-1, keepdims=True)) * EXP2_SCALE)
        norm = jnp.sum(p, axis=-1, keepdims=True)
        p = p.astype(BF)
        split = values[0].shape[0]
        mix = dot(p[:, :split], values[0]) + dot(p[:, split:], values[1])
        out[z] = (mix / norm).astype(BF)


def attend(own, other):
    tok = own.shape[1] // 3
    total = N_Z * tok
    return pl.pallas_call(
        attend_kernel,
        out_shape=sds((N_Z, tok, HEAD_DIM)),
        in_specs=[VMEM] * 2,
        out_specs=VMEM,
        compiler_params=params(12),
        cost_estimate=cost(10 * 10**9, 1024),
        name="attend",
    )(own, other)


def query_kernel(heads, wq, so, cq):
    for h in range(N_Z):
        cols = slice(h * HEAD_DIM, (h + 1) * HEAD_DIM)
        so[:, cols] = heads[h]
        cq[:, cols] = dot(heads[h], wq[h]).astype(BF)


def cross_queries(heads, wq):
    tok = heads.shape[1]
    cols = N_Z * HEAD_DIM
    return pl.pallas_call(
        query_kernel,
        out_shape=[sds((tok, cols))] * 2,
        in_specs=[VMEM] * 2,
        out_specs=[VMEM] * 2,
        compiler_params=params(4),
        cost_estimate=cost(1 * 10**9, 1024),
        name="cross_queries",
    )(heads, wq)


def place_kernel(received, first, second, out):
    rows = jnp.concatenate([received[...], first[...], second[...]], axis=0).astype(F32)
    out[0] = pltpu.roll(rows, rows.shape[0] - 1, 0)[: out.shape[1]].astype(BF)


def place(received, first, second):
    cols = first.shape[1]
    return pl.pallas_call(
        place_kernel,
        out_shape=sds((1, 2 * SPAN, cols)),
        in_specs=[VMEM] * 3,
        out_specs=VMEM,
        compiler_params=params(4),
        cost_estimate=cost(1 * 10**9, 1024),
        name="place",
    )(received, first, second)


def per_device(
    queries, keys_in, values_in, memory, enc_wq, enc_wk, enc_wv, enc_wo,
    cross_wk, cross_wv, cross_wq, nbr_rows, nbr_owner, nbr_count,
):
    idx = (nbr_owner * DB + nbr_rows).reshape(-1)
    asked = [idx] + [shifted(idx, "enc", k) for k in range(1, N_ENC)]
    near, far = to_sides(enc_wo), shifted(enc_wo, "mp", 2)

    packed = over_z(pack(queries, keys_in, values_in))
    sent = fetch(asked, memory)
    received = [sent[0]] + [shifted(sent[k], "enc", -k) for k in range(1, N_ENC)]
    mine = compact(idx, received, (near, far))
    pieces = [mine] + [shifted(mine, "mp", k) for k in range(1, N_MP)]

    packed = after(packed, pieces[1], pieces[3])
    heads = over_z(attend(packed, core_swap(packed)))
    so, cq = cross_queries(heads, cross_wq)

    *values, source = encode(pieces, enc_wq, enc_wk, enc_wv)
    attn = [[v] + [shifted(v, "mp", k) for k in range(1, N_MP)] for v in values]
    wo, wk, wv = load((enc_wo, near, far, core_swap(near)), cross_wk, cross_wv, cq)
    second = cross(1, nbr_count, source, attn[0], wo, wk, wv, cq, so)
    passed = shifted(second, "seq", 1)
    first = cross(0, nbr_count, source, attn[1], wo, wk, wv, cq, so)
    return place(passed, first, second)


def solution(mesh):
    return jax.shard_map(
        per_device,
        mesh=mesh,
        in_specs=(
            P("enc", "seq", "mp"),
            P("enc", "seq", "mp"),
            P("enc", "seq", "mp"),
            P("enc", None, "mp"),
            P(None, "mp"),
            P(None, "mp"),
            P(None, "mp"),
            P("mp", None),
            P(None, "mp"),
            P(None, "mp"),
            P("mp", None, None),
            P("enc", "seq", None),
            P("enc", "seq", None),
            P("enc", None),
        ),
        out_specs=P("enc", "seq", "mp"),
        check_vma=False,
    )
```

```python
import functools
import math

import jax
import jax.numpy as jnp
from jax import lax
from jax.experimental import pallas as pl
from jax.experimental.pallas import tpu as pltpu
from jax.sharding import PartitionSpec as P

HEAD_DIM = 128
SPAN = 64
K_NB = 2
NT = 128
DB = 32
N_ENC = 4
N_MP = 4
N_Z = 8
NEG_BIG = -1e30
SCALE = 1.0 / math.sqrt(HEAD_DIM)
EXP2_SCALE = SCALE * math.log2(math.e)
BF = jnp.bfloat16
F32 = jnp.float32

ANY = pl.BlockSpec(memory_space=pl.ANY)
SMEM = pl.BlockSpec(memory_space=pltpu.SMEM)
VMEM = pl.BlockSpec(memory_space=pltpu.VMEM)
MB = 1024 * 1024


def shifted(block, axis, distance):
    size = lax.axis_size(axis)
    return lax.ppermute(block, axis, [(i, (i + distance) % size) for i in range(size)])


def to_sides(block):
    seqs, mps = lax.axis_size("seq"), lax.axis_size("mp")
    route = [
        (s * mps + m, s * mps + (m + (1 if s % 2 == 0 else -1)) % mps)
        for s in range(seqs)
        for m in range(mps)
    ]
    return lax.ppermute(block, ("seq", "mp"), route)


def core_swap(block):
    size = lax.axis_size("seq")
    return lax.ppermute(block, "seq", [(i, i ^ 1) for i in range(size)])


def over_z(blocks):
    groups = [[2 * z + core for z in range(N_Z)] for core in range(2)]
    return lax.all_to_all(blocks, "seq", 0, 0, axis_index_groups=groups, tiled=True)


def in_hbm(x):
    return pltpu.with_memory_space_constraint(x, pltpu.HBM)


def after(x, *others):
    def kernel(*refs):
        pass

    return pl.pallas_call(
        kernel,
        out_shape=sds(x.shape, x.dtype),
        in_specs=[ANY] * (1 + len(others)),
        out_specs=ANY,
        input_output_aliases={0: 0},
        compiler_params=params(1),
        cost_estimate=cost(0, 1024),
        name="after",
    )(x, *others)


def sds(shape, dtype=BF):
    return jax.ShapeDtypeStruct(shape, dtype)


def params(limit_mb):
    return pltpu.CompilerParams(vmem_limit_bytes=limit_mb * MB)


def cost(flops, nbytes, trans=0):
    return pl.CostEstimate(flops=flops, bytes_accessed=nbytes, transcendentals=trans)


def dot(a, b):
    return jnp.dot(a, b, preferred_element_type=F32)


def dot_t(a, b):
    return lax.dot_general(a, b, (((1,), (1,)), ((), ())), preferred_element_type=F32)


def run_copies(pairs, sems):
    copies = [pltpu.make_async_copy(s, d, sems.at[n]) for n, (s, d) in enumerate(pairs)]
    for c in copies:
        c.start()
    return copies


def fetch_kernel(idx0, idx1, idx2, idx3, memory, s0, s1, s2, s3, sems):
    me = lax.axis_index("enc")
    pairs = []
    for idx, out in ((idx0, s0), (idx1, s1), (idx2, s2), (idx3, s3)):
        for span in range(2):
            row = jnp.int32(0)
            for j in range(K_NB):
                flat = idx[span * K_NB + j]
                row = jnp.where(flat // DB == me, flat % DB, row)
            pairs.append((memory.at[row], out.at[pl.ds(span * NT, NT)]))
    for c in run_copies(pairs, sems):
        c.wait()


def fetch(idx, memory):
    cols = memory.shape[2]
    return pl.pallas_call(
        fetch_kernel,
        out_shape=[sds((2 * NT, cols))] * 4,
        in_specs=[SMEM] * 4 + [ANY],
        out_specs=[ANY] * 4,
        scratch_shapes=[pltpu.SemaphoreType.DMA((8,))],
        compiler_params=params(1),
        cost_estimate=cost(5 * 10**9, 1024),
        name="fetch",
    )(*idx, in_hbm(memory))


def compact_kernel(idx, r0, r1, r2, r3, w1, w2, out, sems):
    me = lax.axis_index("enc")

    def each(act):
        for span in range(2):
            for j in range(K_NB):
                at = (idx[span * K_NB + j] // DB - me + N_ENC) % N_ENC
                for k, r in enumerate((r0, r1, r2, r3)):

                    @pl.when(at == k)
                    def _():
                        act(
                            pltpu.make_async_copy(
                                r.at[pl.ds(span * NT, NT)],
                                out.at[pl.ds((span * K_NB + j) * NT, NT)],
                                sems.at[span * K_NB + j],
                            )
                        )

    each(lambda c: c.start())
    each(lambda c: c.wait())


def compact(idx, received, others):
    rows, cols = received[0].shape
    return pl.pallas_call(
        compact_kernel,
        out_shape=pltpu.HBM((K_NB * rows, cols), BF),
        in_specs=[SMEM] + [ANY] * 6,
        out_specs=ANY,
        scratch_shapes=[pltpu.SemaphoreType.DMA((4,))],
        compiler_params=params(1),
        cost_estimate=cost(1 * 10**9, 1024),
        name="compact",
    )(idx, *received, *others)


def source_columns(k, width):
    col = (lax.axis_index("mp") - k + N_MP) % N_MP
    return pl.ds(pl.multiple_of(col * width, width), width)


def attention(blocks):
    scores = [dot_t(q, k) for q, k, _ in blocks]
    tops = [jnp.max(s, axis=-1, keepdims=True) for s in scores]
    weights = [jnp.exp2((s - m) * EXP2_SCALE) for s, m in zip(scores, tops)]
    mixes = [dot(p.astype(BF), v) for p, (_, _, v) in zip(weights, blocks)]
    totals = [jnp.sum(p, axis=-1, keepdims=True) for p in weights]
    return [mix / total for mix, total in zip(mixes, totals)]


def encode_kernel(x0, x1, x2, x3, wq, wk, wv, first, second, src_out, src, w, sems):
    width = x0.shape[1]
    pairs = [(x, src.at[:, source_columns(k, width)]) for k, x in enumerate((x0, x1, x2, x3))]
    pairs += [(ref, w.at[n]) for n, ref in enumerate((wq, wk, wv))]
    copies = run_copies(pairs, sems)
    for c in copies[:5]:
        c.wait()
    kept = pltpu.make_async_copy(src, src_out, sems.at[0])
    kept.start()
    source = src[...]
    q = dot(source, w[0]).astype(BF)
    copies[5].wait()
    k = dot(source, w[1]).astype(BF)
    copies[6].wait()
    v = dot(source, w[2]).astype(BF)
    places = [
        (slice(n * NT, (n + 1) * NT), slice(h * HEAD_DIM, (h + 1) * HEAD_DIM))
        for n in range(src.shape[0] // NT)
        for h in range(width // HEAD_DIM)
    ]
    for at, mix in zip(places, attention([(q[at], k[at], v[at]) for at in places])):
        rows, cols = at
        out = (first, second)[rows.start // (K_NB * NT)]
        begin = rows.start % (K_NB * NT)
        out[begin : begin + NT, cols] = mix.astype(BF)
    kept.wait()


def encode(pieces, wq, wk, wv):
    rows, width = pieces[0].shape
    depth = wq.shape[0]
    return pl.pallas_call(
        encode_kernel,
        out_shape=[sds((rows // 2, width))] * 2 + [pltpu.HBM((rows, depth), BF)],
        in_specs=[ANY] * 7,
        out_specs=[VMEM, VMEM, ANY],
        scratch_shapes=[
            pltpu.VMEM((rows, depth), BF),
            pltpu.VMEM((3, depth, width), BF),
            pltpu.SemaphoreType.DMA((7,)),
        ],
        compiler_params=params(12),
        cost_estimate=cost(30 * 10**9, 1024),
        name="encode",
    )(*pieces, *map(in_hbm, (wq, wk, wv)))


def load_kernel(w0, w_near, w_half, s_near, s_half, tie, wo_out, sems):
    width = w0.shape[0]
    half = width // 2
    core = lax.axis_index("seq") % 2
    begins = [(w0, 0), (w_near, (1 + 2 * core) * width), (s_near, (3 - 2 * core) * width)]
    begins += [(w_half, 2 * width + core * half), (s_half, 2 * width + (1 - core) * half)]
    pairs = []
    for w, begin in begins:
        rows = w.shape[0]
        pairs.append((w, wo_out.at[pl.ds(pl.multiple_of(begin, half), rows)]))
    for c in run_copies(pairs, sems):
        c.wait()


def load(wo, tie):
    depth = wo[0].shape[1]
    return pl.pallas_call(
        load_kernel,
        out_shape=pltpu.VMEM((depth, depth), BF),
        in_specs=[ANY] * 6,
        out_specs=ANY,
        scratch_shapes=[pltpu.SemaphoreType.DMA((5,))],
        compiler_params=params(1),
        cost_estimate=cost(3 * 10**9, 1024),
        name="load",
    )(*map(in_hbm, wo), tie)


def cross_kernel(which, counts, src, a0, a1, a2, a3, wo, wk, wv, cq, so, out, src_s, attn, sems):
    nbrs, width = a0.shape
    pairs = [(a, attn.at[:, pl.ds(k * width, width)]) for k, a in enumerate((a0, a1, a2, a3))]
    copies = run_copies(pairs + [(src.at[pl.ds(which * nbrs, nbrs)], src_s)], sems)
    seq = lax.axis_index("seq")
    count = counts[0, seq * 2 + which]
    shape = (SPAN, nbrs)
    alive = lax.broadcasted_iota(jnp.int32, shape, 1) < count * NT
    if which == 1:
        past = (lax.broadcasted_iota(jnp.int32, shape, 0) > 0) & (seq == lax.axis_size("seq") - 1)
        alive = alive & jnp.logical_not(past)
    for c in copies[:4]:
        c.wait()
    mixed = dot(attn[...], wo[...])
    copies[4].wait()
    encoded = (src_s[...].astype(F32) + mixed).astype(BF)
    keys = dot(encoded, wk[...]).astype(BF)
    values = dot(encoded, wv[...]).astype(BF)
    rows = slice(which * SPAN, (which + 1) * SPAN)
    heads = [slice(h * HEAD_DIM, (h + 1) * HEAD_DIM) for h in range(cq.shape[1] // HEAD_DIM)]
    scores = [jnp.where(alive, dot_t(cq[rows, c], keys[:, c]), NEG_BIG) for c in heads]
    tops = [jnp.max(s, axis=-1, keepdims=True) for s in scores]
    weights = [jnp.exp2((s - m) * EXP2_SCALE) for s, m in zip(scores, tops)]
    weights = [jnp.where(alive, p, 0.0) for p in weights]
    mixes = [dot(p.astype(BF), values[:, c]) for p, c in zip(weights, heads)]
    totals = [jnp.sum(p, axis=-1, keepdims=True) for p in weights]
    for c, mix, total in zip(heads, mixes, totals):
        out[:, c] = (so[rows, c].astype(F32) + mix / jnp.maximum(total, 1.0)).astype(BF)


def cross(which, counts, source, attn, wo, wk, wv, cq, so):
    rows, depth = source.shape
    cols = cq.shape[1]

    def body(*refs):
        cross_kernel(which, *refs)

    return pl.pallas_call(
        body,
        out_shape=sds((SPAN, cols)),
        in_specs=[SMEM] + [ANY] * 5 + [VMEM] * 5,
        out_specs=VMEM,
        scratch_shapes=[
            pltpu.VMEM((rows // 2, depth), BF),
            pltpu.VMEM((rows // 2, depth), BF),
            pltpu.SemaphoreType.DMA((5,)),
        ],
        compiler_params=params(12),
        cost_estimate=cost(5 * 10**9, 1024),
        name="cross",
    )(counts, in_hbm(source), *attn, wo, wk, wv, cq, so)


def pack_kernel(q, k, v, wo, nbr_rows, nbr_owner, out, idx, half, rows, at_row, at_owner, sems):
    tok = q.shape[1]
    places = run_copies([(nbr_rows, at_row), (nbr_owner, at_owner)], sems)
    pairs = [(ref.at[0], rows.at[n]) for n, ref in enumerate((q, k, v))]
    count = half.shape[0]
    core = lax.axis_index("seq") % 2
    pairs.append((wo.at[pl.ds(pl.multiple_of(core * count, count), count)], half))
    copies = run_copies(pairs, sems.at[pl.ds(2, 4)])
    for c in places:
        c.wait()
    for span in range(2):
        for j in range(K_NB):
            idx[span * K_NB + j] = at_owner[0, span, j] * DB + at_row[0, span, j]
    for n, c in enumerate(copies[:3]):
        c.wait()
        for head in range(N_Z):
            cols = slice(head * HEAD_DIM, (head + 1) * HEAD_DIM)
            out[head, n * tok : (n + 1) * tok, :] = rows[n, :, cols]
    copies[3].wait()


def pack(q, k, v, wo, nbr_rows, nbr_owner):
    _, tok, cols = q.shape
    return pl.pallas_call(
        pack_kernel,
        out_shape=[
            sds((N_Z, 3 * tok, HEAD_DIM)),
            sds((2 * K_NB,), jnp.int32),
            sds((wo.shape[0] // 2, wo.shape[1])),
        ],
        in_specs=[ANY] * 6,
        out_specs=[VMEM, SMEM, VMEM],
        scratch_shapes=[
            pltpu.VMEM((3, tok, cols), BF),
            pltpu.SMEM(nbr_rows.shape, jnp.int32),
            pltpu.SMEM(nbr_owner.shape, jnp.int32),
            pltpu.SemaphoreType.DMA((6,)),
        ],
        compiler_params=params(4),
        cost_estimate=cost(10**9, 1024),
        name="pack",
    )(*map(in_hbm, (q, k, v, wo, nbr_rows, nbr_owner)))


def attend_kernel(own, other, out):
    core = lax.axis_index("seq") % 2
    tok = out.shape[1]
    tokens = 2 * N_Z * tok

    def block_parts(z):
        after_z = (z + 1) % N_Z
        nxt = jnp.where(core == 0, other[z, :SPAN].astype(F32), other[after_z, :SPAN].astype(F32))
        both = jnp.concatenate([own[z, :tok].astype(F32), nxt], axis=0)
        rolled = pltpu.roll(both, both.shape[0] - (SPAN - 1), 0)[:tok].astype(BF)
        pos = (2 * z + core) * tok + SPAN - 1 + lax.broadcasted_iota(jnp.int32, (tok, 1), 0)
        pos = jnp.where(pos >= tokens, pos - tokens, pos)
        col = lax.broadcasted_iota(jnp.int32, (1, tok), 1)
        parts, values = [], []
        for n, ref, parity in ((z + 1, own, core), (min(z + 2, N_Z), other, 1 - core)):
            s = dot_t(rolled, ref[:n, tok : 2 * tok].reshape(n * tok, HEAD_DIM))
            values.append(ref[:n, 2 * tok :].reshape(n * tok, HEAD_DIM))
            for b in range(n):
                piece = s[:, b * tok : (b + 1) * tok]
                if b >= z or z == N_Z - 1:
                    piece = jnp.where((2 * b + parity) * tok + col <= pos, piece, NEG_BIG)
                parts.append(piece)
        return parts, values

    for group in ((0, 7, 3, 4), (1, 6, 2, 5)):
        made = [block_parts(z) for z in group]
        tops = [jnp.max(functools.reduce(jnp.maximum, parts), axis=-1, keepdims=True) for parts, _ in made]
        weights = [[jnp.exp2((s - m) * EXP2_SCALE) for s in parts] for (parts, _), m in zip(made, tops)]
        totals = [jnp.sum(functools.reduce(jnp.add, ps), axis=-1, keepdims=True) for ps in weights]
        mixes = []
        for ps, (_, (mine, theirs)) in zip(weights, made):
            p = jnp.concatenate([part.astype(BF) for part in ps], axis=1)
            split = mine.shape[0]
            mixes.append(dot(p[:, :split], mine) + dot(p[:, split:], theirs))
        for z, mix, total in zip(group, mixes, totals):
            out[z] = (mix / total).astype(BF)


def attend(own, other):
    tok = own.shape[1] // 3
    total = N_Z * tok
    return pl.pallas_call(
        attend_kernel,
        out_shape=sds((N_Z, tok, HEAD_DIM)),
        in_specs=[VMEM] * 2,
        out_specs=VMEM,
        compiler_params=params(12),
        cost_estimate=cost(10 * 10**9, 1024),
        name="attend",
    )(own, other)


def query_kernel(heads, wq, so, cq):
    for h in range(N_Z):
        cols = slice(h * HEAD_DIM, (h + 1) * HEAD_DIM)
        so[:, cols] = heads[h]
        cq[:, cols] = dot(heads[h], wq[h]).astype(BF)


def cross_queries(heads, wq):
    tok = heads.shape[1]
    cols = N_Z * HEAD_DIM
    return pl.pallas_call(
        query_kernel,
        out_shape=[sds((tok, cols))] * 2,
        in_specs=[VMEM] * 2,
        out_specs=[VMEM] * 2,
        compiler_params=params(4),
        cost_estimate=cost(1 * 10**9, 1024),
        name="cross_queries",
    )(heads, wq)


def place_kernel(received, first, second, out):
    rows = jnp.concatenate([received[...], first[...], second[...]], axis=0).astype(F32)
    out[0] = pltpu.roll(rows, rows.shape[0] - 1, 0)[: out.shape[1]].astype(BF)


def place(received, first, second):
    cols = first.shape[1]
    return pl.pallas_call(
        place_kernel,
        out_shape=sds((1, 2 * SPAN, cols)),
        in_specs=[VMEM] * 3,
        out_specs=VMEM,
        compiler_params=params(4),
        cost_estimate=cost(1 * 10**9, 1024),
        name="place",
    )(received, first, second)


def per_device(
    queries, keys_in, values_in, memory, enc_wq, enc_wk, enc_wv, enc_wo,
    cross_wk, cross_wv, cross_wq, nbr_rows, nbr_owner, nbr_count,
):
    packed, idx, wo_half = pack(queries, keys_in, values_in, enc_wo, nbr_rows, nbr_owner)
    packed = over_z(packed)
    asked = [idx] + [shifted(idx, "enc", k) for k in range(1, N_ENC)]
    near, far = to_sides(enc_wo), shifted(wo_half, "mp", 2)

    sent = fetch(asked, memory)
    received = [sent[0]] + [shifted(sent[k], "enc", -k) for k in range(1, N_ENC)]
    mine = compact(idx, received, (near, far))
    pieces = [mine] + [shifted(mine, "mp", k) for k in range(1, N_MP)]

    packed = after(packed, in_hbm(mine))
    heads = over_z(attend(packed, core_swap(packed)))
    so, cq = cross_queries(heads, cross_wq)

    early, late, source = encode(pieces, enc_wq, enc_wk, enc_wv)
    late = [late] + [shifted(late, "mp", k) for k in range(1, N_MP)]
    early = after(early, late[1])
    early = [early] + [shifted(early, "mp", k) for k in range(1, N_MP)]
    wo = load((enc_wo, near, far, core_swap(near), core_swap(far)), cq)
    second = cross(1, nbr_count, source, late, wo, cross_wk, cross_wv, cq, so)
    passed = shifted(second, "seq", 1)
    first = cross(0, nbr_count, source, early, wo, cross_wk, cross_wv, cq, so)
    return place(passed, first, second)


def solution(mesh):
    return jax.shard_map(
        per_device,
        mesh=mesh,
        in_specs=(
            P("enc", "seq", "mp"),
            P("enc", "seq", "mp"),
            P("enc", "seq", "mp"),
            P("enc", None, "mp"),
            P(None, "mp"),
            P(None, "mp"),
            P(None, "mp"),
            P("mp", None),
            P(None, "mp"),
            P(None, "mp"),
            P("mp", None, None),
            P("enc", "seq", None),
            P("enc", "seq", None),
            P("enc", None),
        ),
        out_specs=P("enc", "seq", "mp"),
        check_vma=False,
    )
```

```python
import functools
import math

import jax
import jax.numpy as jnp
from jax import lax
from jax.experimental import pallas as pl
from jax.experimental.pallas import tpu as pltpu
from jax.sharding import PartitionSpec as P

HEAD_DIM = 128
SPAN = 64
K_NB = 2
NT = 128
DB = 32
N_ENC = 4
N_MP = 4
N_Z = 8
NEG_BIG = -1e30
SCALE = 1.0 / math.sqrt(HEAD_DIM)
EXP2_SCALE = SCALE * math.log2(math.e)
BF = jnp.bfloat16
F32 = jnp.float32

ANY = pl.BlockSpec(memory_space=pl.ANY)
SMEM = pl.BlockSpec(memory_space=pltpu.SMEM)
VMEM = pl.BlockSpec(memory_space=pltpu.VMEM)
MB = 1024 * 1024


def shifted(block, axis, distance):
    size = lax.axis_size(axis)
    return lax.ppermute(block, axis, [(i, (i + distance) % size) for i in range(size)])


def to_sides(block):
    seqs, mps = lax.axis_size("seq"), lax.axis_size("mp")
    route = [
        (s * mps + m, s * mps + (m + (1 if s % 2 == 0 else -1)) % mps)
        for s in range(seqs)
        for m in range(mps)
    ]
    return lax.ppermute(block, ("seq", "mp"), route)


def core_swap(block):
    size = lax.axis_size("seq")
    return lax.ppermute(block, "seq", [(i, i ^ 1) for i in range(size)])


def over_z(blocks):
    groups = [[2 * z + core for z in range(N_Z)] for core in range(2)]
    return lax.all_to_all(blocks, "seq", 0, 0, axis_index_groups=groups, tiled=True)


def in_hbm(x):
    return pltpu.with_memory_space_constraint(x, pltpu.HBM)


def after(x, *others):
    def kernel(*refs):
        pass

    return pl.pallas_call(
        kernel,
        out_shape=sds(x.shape, x.dtype),
        in_specs=[ANY] * (1 + len(others)),
        out_specs=ANY,
        input_output_aliases={0: 0},
        compiler_params=params(1),
        cost_estimate=cost(0, 1024),
        name="after",
    )(x, *others)


def sds(shape, dtype=BF):
    return jax.ShapeDtypeStruct(shape, dtype)


def params(limit_mb):
    return pltpu.CompilerParams(vmem_limit_bytes=limit_mb * MB)


def cost(flops, nbytes, trans=0):
    return pl.CostEstimate(flops=flops, bytes_accessed=nbytes, transcendentals=trans)


def dot(a, b):
    return jnp.dot(a, b, preferred_element_type=F32)


def dot_t(a, b):
    return lax.dot_general(a, b, (((1,), (1,)), ((), ())), preferred_element_type=F32)


def run_copies(pairs, sems):
    copies = [pltpu.make_async_copy(s, d, sems.at[n]) for n, (s, d) in enumerate(pairs)]
    for c in copies:
        c.start()
    return copies


def fetch_kernel(idx0, idx1, idx2, idx3, memory, s0, s1, s2, s3, sems):
    me = lax.axis_index("enc")
    pairs = []
    for idx, out in ((idx0, s0), (idx1, s1), (idx2, s2), (idx3, s3)):
        for span in range(2):
            row = jnp.int32(0)
            for j in range(K_NB):
                flat = idx[span * K_NB + j]
                row = jnp.where(flat // DB == me, flat % DB, row)
            pairs.append((memory.at[row], out.at[pl.ds(span * NT, NT)]))
    for c in run_copies(pairs, sems):
        c.wait()


def fetch(idx, memory):
    cols = memory.shape[2]
    return pl.pallas_call(
        fetch_kernel,
        out_shape=[sds((2 * NT, cols))] * 4,
        in_specs=[SMEM] * 4 + [ANY],
        out_specs=[ANY] * 4,
        scratch_shapes=[pltpu.SemaphoreType.DMA((8,))],
        compiler_params=params(1),
        cost_estimate=cost(5 * 10**9, 1024),
        name="fetch",
    )(*idx, in_hbm(memory))


def compact_kernel(idx, r0, r1, r2, r3, w1, w2, out, sems):
    me = lax.axis_index("enc")

    def each(act):
        for span in range(2):
            for j in range(K_NB):
                at = (idx[span * K_NB + j] // DB - me + N_ENC) % N_ENC
                for k, r in enumerate((r0, r1, r2, r3)):

                    @pl.when(at == k)
                    def _():
                        act(
                            pltpu.make_async_copy(
                                r.at[pl.ds(span * NT, NT)],
                                out.at[pl.ds((span * K_NB + j) * NT, NT)],
                                sems.at[span * K_NB + j],
                            )
                        )

    each(lambda c: c.start())
    each(lambda c: c.wait())


def compact(idx, received, others):
    rows, cols = received[0].shape
    return pl.pallas_call(
        compact_kernel,
        out_shape=sds((K_NB * rows, cols)),
        in_specs=[SMEM] + [ANY] * 6,
        out_specs=ANY,
        scratch_shapes=[pltpu.SemaphoreType.DMA((4,))],
        compiler_params=params(1),
        cost_estimate=cost(1 * 10**9, 1024),
        name="compact",
    )(idx, *received, *others)


def source_columns(k, width):
    col = (lax.axis_index("mp") - k + N_MP) % N_MP
    return pl.ds(pl.multiple_of(col * width, width), width)


def attention(blocks):
    scores = [dot_t(q, k) for q, k, _ in blocks]
    tops = [jnp.max(s, axis=-1, keepdims=True) for s in scores]
    weights = [jnp.exp2((s - m) * EXP2_SCALE) for s, m in zip(scores, tops)]
    mixes = [dot(p.astype(BF), v) for p, (_, _, v) in zip(weights, blocks)]
    totals = [jnp.sum(p, axis=-1, keepdims=True) for p in weights]
    return [mix / total for mix, total in zip(mixes, totals)]


def encode_kernel(x0, x1, x2, x3, wq, wk, wv, first, second, src_out, src, sems):
    width = x0.shape[1]
    pairs = [(x, src.at[:, source_columns(k, width)]) for k, x in enumerate((x0, x1, x2, x3))]
    for c in run_copies(pairs, sems):
        c.wait()
    kept = pltpu.make_async_copy(src, src_out, sems.at[0])
    kept.start()
    source = src[...]
    q, k, v = (dot(source, w[...]).astype(BF) for w in (wq, wk, wv))
    places = [
        (slice(n * NT, (n + 1) * NT), slice(h * HEAD_DIM, (h + 1) * HEAD_DIM))
        for n in range(src.shape[0] // NT)
        for h in range(width // HEAD_DIM)
    ]
    for at, mix in zip(places, attention([(q[at], k[at], v[at]) for at in places])):
        rows, cols = at
        out = (first, second)[rows.start // (K_NB * NT)]
        begin = rows.start % (K_NB * NT)
        out[begin : begin + NT, cols] = mix.astype(BF)
    kept.wait()


def encode(pieces, wq, wk, wv):
    rows, width = pieces[0].shape
    depth = wq.shape[0]
    return pl.pallas_call(
        encode_kernel,
        out_shape=[sds((rows // 2, width))] * 2 + [pltpu.HBM((rows, depth), BF)],
        in_specs=[ANY] * 4 + [VMEM] * 3,
        out_specs=[VMEM, VMEM, ANY],
        scratch_shapes=[pltpu.VMEM((rows, depth), BF), pltpu.SemaphoreType.DMA((4,))],
        compiler_params=params(12),
        cost_estimate=cost(30 * 10**9, 1024),
        name="encode",
    )(*pieces, wq, wk, wv)


def load_kernel(w0, w_near, w_half, s_near, s_half, tie, wo_out, sems):
    width = w0.shape[0]
    half = width // 2
    core = lax.axis_index("seq") % 2
    begins = [(w0, 0), (w_near, (1 + 2 * core) * width), (s_near, (3 - 2 * core) * width)]
    begins += [(w_half, 2 * width + core * half), (s_half, 2 * width + (1 - core) * half)]
    pairs = []
    for w, begin in begins:
        rows = w.shape[0]
        pairs.append((w, wo_out.at[pl.ds(pl.multiple_of(begin, half), rows)]))
    for c in run_copies(pairs, sems):
        c.wait()


def load(wo, tie):
    depth = wo[0].shape[1]
    return pl.pallas_call(
        load_kernel,
        out_shape=pltpu.VMEM((depth, depth), BF),
        in_specs=[ANY] * 6,
        out_specs=ANY,
        scratch_shapes=[pltpu.SemaphoreType.DMA((5,))],
        compiler_params=params(1),
        cost_estimate=cost(3 * 10**9, 1024),
        name="load",
    )(*map(in_hbm, wo[:3]), *wo[3:], tie)


def cross_kernel(which, counts, src, a0, a1, a2, a3, wo, wk, wv, cq, so, out, src_s, attn, sems):
    nbrs, width = a0.shape
    pairs = [(a, attn.at[:, pl.ds(k * width, width)]) for k, a in enumerate((a0, a1, a2, a3))]
    copies = run_copies(pairs + [(src.at[pl.ds(which * nbrs, nbrs)], src_s)], sems)
    seq = lax.axis_index("seq")
    count = counts[0, seq * 2 + which]
    shape = (SPAN, nbrs)
    alive = lax.broadcasted_iota(jnp.int32, shape, 1) < count * NT
    if which == 1:
        past = (lax.broadcasted_iota(jnp.int32, shape, 0) > 0) & (seq == lax.axis_size("seq") - 1)
        alive = alive & jnp.logical_not(past)
    for c in copies[:4]:
        c.wait()
    mixed = dot(attn[...], wo[...])
    copies[4].wait()
    encoded = (src_s[...].astype(F32) + mixed).astype(BF)
    keys = dot(encoded, wk[...]).astype(BF)
    values = dot(encoded, wv[...]).astype(BF)
    rows = slice(which * SPAN, (which + 1) * SPAN)
    heads = [slice(h * HEAD_DIM, (h + 1) * HEAD_DIM) for h in range(cq.shape[1] // HEAD_DIM)]
    scores = [jnp.where(alive, dot_t(cq[rows, c], keys[:, c]), NEG_BIG) for c in heads]
    tops = [jnp.max(s, axis=-1, keepdims=True) for s in scores]
    weights = [jnp.exp2((s - m) * EXP2_SCALE) for s, m in zip(scores, tops)]
    weights = [jnp.where(alive, p, 0.0) for p in weights]
    mixes = [dot(p.astype(BF), values[:, c]) for p, c in zip(weights, heads)]
    totals = [jnp.sum(p, axis=-1, keepdims=True) for p in weights]
    for c, mix, total in zip(heads, mixes, totals):
        out[:, c] = (so[rows, c].astype(F32) + mix / jnp.maximum(total, 1.0)).astype(BF)


def cross(which, counts, source, attn, wo, wk, wv, cq, so):
    rows, depth = source.shape
    cols = cq.shape[1]

    def body(*refs):
        cross_kernel(which, *refs)

    return pl.pallas_call(
        body,
        out_shape=sds((SPAN, cols)),
        in_specs=[SMEM] + [ANY] * 5 + [VMEM] * 5,
        out_specs=VMEM,
        scratch_shapes=[
            pltpu.VMEM((rows // 2, depth), BF),
            pltpu.VMEM((rows // 2, depth), BF),
            pltpu.SemaphoreType.DMA((5,)),
        ],
        compiler_params=params(12),
        cost_estimate=cost(5 * 10**9, 1024),
        name="cross",
    )(counts, in_hbm(source), *attn, wo, wk, wv, cq, so)


def pack_kernel(q, k, v, wo, nbr_rows, nbr_owner, out, idx, half, rows, at_row, at_owner, sems):
    tok = q.shape[1]
    places = run_copies([(nbr_rows, at_row), (nbr_owner, at_owner)], sems)
    pairs = [(ref.at[0], rows.at[n]) for n, ref in enumerate((q, k, v))]
    count = half.shape[0]
    core = lax.axis_index("seq") % 2
    pairs.append((wo.at[pl.ds(pl.multiple_of(core * count, count), count)], half))
    copies = run_copies(pairs, sems.at[pl.ds(2, 4)])
    for c in places:
        c.wait()
    for span in range(2):
        for j in range(K_NB):
            idx[span * K_NB + j] = at_owner[0, span, j] * DB + at_row[0, span, j]
    for n, c in enumerate(copies[:3]):
        c.wait()
        for head in range(N_Z):
            cols = slice(head * HEAD_DIM, (head + 1) * HEAD_DIM)
            out[head, n * tok : (n + 1) * tok, :] = rows[n, :, cols]
    copies[3].wait()


def pack(q, k, v, wo, nbr_rows, nbr_owner):
    _, tok, cols = q.shape
    return pl.pallas_call(
        pack_kernel,
        out_shape=[
            sds((N_Z, 3 * tok, HEAD_DIM)),
            sds((2 * K_NB,), jnp.int32),
            sds((wo.shape[0] // 2, wo.shape[1])),
        ],
        in_specs=[ANY] * 6,
        out_specs=[VMEM, SMEM, VMEM],
        scratch_shapes=[
            pltpu.VMEM((3, tok, cols), BF),
            pltpu.SMEM(nbr_rows.shape, jnp.int32),
            pltpu.SMEM(nbr_owner.shape, jnp.int32),
            pltpu.SemaphoreType.DMA((6,)),
        ],
        compiler_params=params(4),
        cost_estimate=cost(10**9, 1024),
        name="pack",
    )(*map(in_hbm, (q, k, v, wo, nbr_rows, nbr_owner)))


def attend_kernel(own, other, out):
    core = lax.axis_index("seq") % 2
    tok = out.shape[1]
    tokens = 2 * N_Z * tok

    def block_parts(z):
        after_z = (z + 1) % N_Z
        nxt = jnp.where(core == 0, other[z, :SPAN].astype(F32), other[after_z, :SPAN].astype(F32))
        both = jnp.concatenate([own[z, :tok].astype(F32), nxt], axis=0)
        rolled = pltpu.roll(both, both.shape[0] - (SPAN - 1), 0)[:tok].astype(BF)
        pos = (2 * z + core) * tok + SPAN - 1 + lax.broadcasted_iota(jnp.int32, (tok, 1), 0)
        pos = jnp.where(pos >= tokens, pos - tokens, pos)
        col = lax.broadcasted_iota(jnp.int32, (1, tok), 1)
        parts, values = [], []
        for n, ref, parity in ((z + 1, own, core), (min(z + 2, N_Z), other, 1 - core)):
            s = dot_t(rolled, ref[:n, tok : 2 * tok].reshape(n * tok, HEAD_DIM))
            values.append(ref[:n, 2 * tok :].reshape(n * tok, HEAD_DIM))
            for b in range(n):
                piece = s[:, b * tok : (b + 1) * tok]
                if b >= z or z == N_Z - 1:
                    piece = jnp.where((2 * b + parity) * tok + col <= pos, piece, NEG_BIG)
                parts.append(piece)
        return parts, values

    for group in ((0, 7, 3, 4), (1, 6, 2, 5)):
        made = [block_parts(z) for z in group]
        tops = [jnp.max(functools.reduce(jnp.maximum, parts), axis=-1, keepdims=True) for parts, _ in made]
        weights = [[jnp.exp2((s - m) * EXP2_SCALE) for s in parts] for (parts, _), m in zip(made, tops)]
        totals = [jnp.sum(functools.reduce(jnp.add, ps), axis=-1, keepdims=True) for ps in weights]
        mixes = []
        for ps, (_, (mine, theirs)) in zip(weights, made):
            p = jnp.concatenate([part.astype(BF) for part in ps], axis=1)
            split = mine.shape[0]
            mixes.append(dot(p[:, :split], mine) + dot(p[:, split:], theirs))
        for z, mix, total in zip(group, mixes, totals):
            out[z] = (mix / total).astype(BF)


def attend(own, other):
    tok = own.shape[1] // 3
    total = N_Z * tok
    return pl.pallas_call(
        attend_kernel,
        out_shape=sds((N_Z, tok, HEAD_DIM)),
        in_specs=[VMEM] * 2,
        out_specs=VMEM,
        compiler_params=params(12),
        cost_estimate=cost(10 * 10**9, 1024),
        name="attend",
    )(own, other)


def query_kernel(heads, wq, so, cq):
    for h in range(N_Z):
        cols = slice(h * HEAD_DIM, (h + 1) * HEAD_DIM)
        so[:, cols] = heads[h]
        cq[:, cols] = dot(heads[h], wq[h]).astype(BF)


def cross_queries(heads, wq):
    tok = heads.shape[1]
    cols = N_Z * HEAD_DIM
    return pl.pallas_call(
        query_kernel,
        out_shape=[sds((tok, cols))] * 2,
        in_specs=[VMEM] * 2,
        out_specs=[VMEM] * 2,
        compiler_params=params(4),
        cost_estimate=cost(1 * 10**9, 1024),
        name="cross_queries",
    )(heads, wq)


def place_kernel(received, first, second, out):
    rows = jnp.concatenate([received[...], first[...], second[...]], axis=0).astype(F32)
    out[0] = pltpu.roll(rows, rows.shape[0] - 1, 0)[: out.shape[1]].astype(BF)


def place(received, first, second):
    cols = first.shape[1]
    return pl.pallas_call(
        place_kernel,
        out_shape=sds((1, 2 * SPAN, cols)),
        in_specs=[VMEM] * 3,
        out_specs=VMEM,
        compiler_params=params(4),
        cost_estimate=cost(1 * 10**9, 1024),
        name="place",
    )(received, first, second)


def per_device(
    queries, keys_in, values_in, memory, enc_wq, enc_wk, enc_wv, enc_wo,
    cross_wk, cross_wv, cross_wq, nbr_rows, nbr_owner, nbr_count,
):
    packed, idx, wo_half = pack(queries, keys_in, values_in, enc_wo, nbr_rows, nbr_owner)
    packed = over_z(packed)
    asked = [idx] + [shifted(idx, "enc", k) for k in range(1, N_ENC)]
    near, far = to_sides(enc_wo), shifted(wo_half, "mp", 2)

    sent = fetch(asked, memory)
    received = [sent[0]] + [shifted(sent[k], "enc", -k) for k in range(1, N_ENC)]
    mine = compact(idx, received, (near, far))
    pieces = [mine] + [shifted(mine, "mp", k) for k in range(1, N_MP)]

    packed = after(packed, mine)
    heads = over_z(attend(packed, core_swap(packed)))
    so, cq = cross_queries(heads, cross_wq)

    early, late, source = encode(pieces, enc_wq, enc_wk, enc_wv)
    late = [late] + [shifted(late, "mp", k) for k in range(1, N_MP)]
    wo = load((enc_wo, near, far, core_swap(near), core_swap(far)), cq)
    early = after(early, wo)
    early = [early] + [shifted(early, "mp", k) for k in range(1, N_MP)]
    second = cross(1, nbr_count, source, late, wo, cross_wk, cross_wv, cq, so)
    passed = shifted(second, "seq", 1)
    first = cross(0, nbr_count, source, early, wo, cross_wk, cross_wv, cq, so)
    return place(passed, first, second)


def solution(mesh):
    return jax.shard_map(
        per_device,
        mesh=mesh,
        in_specs=(
            P("enc", "seq", "mp"),
            P("enc", "seq", "mp"),
            P("enc", "seq", "mp"),
            P("enc", None, "mp"),
            P(None, "mp"),
            P(None, "mp"),
            P(None, "mp"),
            P("mp", None),
            P(None, "mp"),
            P(None, "mp"),
            P("mp", None, None),
            P("enc", "seq", None),
            P("enc", "seq", None),
            P("enc", None),
        ),
        out_specs=P("enc", "seq", "mp"),
        check_vma=False,
    )
```

```python
import functools
import math

import jax
import jax.numpy as jnp
from jax import lax
from jax.experimental import pallas as pl
from jax.experimental.pallas import tpu as pltpu
from jax.sharding import PartitionSpec as P

HEAD_DIM = 128
SPAN = 64
K_NB = 2
NT = 128
DB = 32
N_ENC = 4
N_MP = 4
N_Z = 8
NEG_BIG = -1e30
SCALE = 1.0 / math.sqrt(HEAD_DIM)
EXP2_SCALE = SCALE * math.log2(math.e)
BF = jnp.bfloat16
F32 = jnp.float32

ANY = pl.BlockSpec(memory_space=pl.ANY)
SMEM = pl.BlockSpec(memory_space=pltpu.SMEM)
VMEM = pl.BlockSpec(memory_space=pltpu.VMEM)
MB = 1024 * 1024


def shifted(block, axis, distance):
    size = lax.axis_size(axis)
    return lax.ppermute(block, axis, [(i, (i + distance) % size) for i in range(size)])


def to_sides(block):
    seqs, mps = lax.axis_size("seq"), lax.axis_size("mp")
    route = [
        (s * mps + m, s * mps + (m + (1 if s % 2 == 0 else -1)) % mps)
        for s in range(seqs)
        for m in range(mps)
    ]
    return lax.ppermute(block, ("seq", "mp"), route)


def core_swap(block):
    size = lax.axis_size("seq")
    return lax.ppermute(block, "seq", [(i, i ^ 1) for i in range(size)])


def turned(z):
    return (z + 1) % N_Z


def over_z(blocks):
    groups = [[2 * (n - 1) % (2 * N_Z) + core for n in range(N_Z)] for core in range(2)]
    return lax.all_to_all(blocks, "seq", 0, 0, axis_index_groups=groups, tiled=True)


def in_hbm(x):
    return pltpu.with_memory_space_constraint(x, pltpu.HBM)


def after(x, *others):
    def kernel(*refs):
        pass

    return pl.pallas_call(
        kernel,
        out_shape=sds(x.shape, x.dtype),
        in_specs=[ANY] * (1 + len(others)),
        out_specs=ANY,
        input_output_aliases={0: 0},
        compiler_params=params(1),
        cost_estimate=cost(0, 1024),
        name="after",
    )(x, *others)


def sds(shape, dtype=BF):
    return jax.ShapeDtypeStruct(shape, dtype)


def params(limit_mb):
    return pltpu.CompilerParams(vmem_limit_bytes=limit_mb * MB)


def cost(flops, nbytes, trans=0):
    return pl.CostEstimate(flops=flops, bytes_accessed=nbytes, transcendentals=trans)


def dot(a, b):
    return jnp.dot(a, b, preferred_element_type=F32)


def dot_t(a, b):
    return lax.dot_general(a, b, (((1,), (1,)), ((), ())), preferred_element_type=F32)


def run_copies(pairs, sems):
    copies = [pltpu.make_async_copy(s, d, sems.at[n]) for n, (s, d) in enumerate(pairs)]
    for c in copies:
        c.start()
    return copies


def fetch_kernel(idx0, idx1, idx2, idx3, memory, s0, s1, s2, s3, sems):
    me = lax.axis_index("enc")
    pairs = []
    for idx, out in ((idx0, s0), (idx1, s1), (idx2, s2), (idx3, s3)):
        for span in range(2):
            row = jnp.int32(0)
            for j in range(K_NB):
                flat = idx[span * K_NB + j]
                row = jnp.where(flat // DB == me, flat % DB, row)
            pairs.append((memory.at[row], out.at[pl.ds(span * NT, NT)]))
    for c in run_copies(pairs, sems):
        c.wait()


def fetch(idx, memory):
    cols = memory.shape[2]
    return pl.pallas_call(
        fetch_kernel,
        out_shape=[sds((2 * NT, cols))] * 4,
        in_specs=[SMEM] * 4 + [ANY],
        out_specs=[ANY] * 4,
        scratch_shapes=[pltpu.SemaphoreType.DMA((8,))],
        compiler_params=params(1),
        cost_estimate=cost(5 * 10**9, 1024),
        name="fetch",
    )(*idx, in_hbm(memory))


def compact_kernel(idx, r0, r1, r2, r3, w1, w2, out, sems):
    me = lax.axis_index("enc")

    def each(act):
        for span in range(2):
            for j in range(K_NB):
                at = (idx[span * K_NB + j] // DB - me + N_ENC) % N_ENC
                for k, r in enumerate((r0, r1, r2, r3)):

                    @pl.when(at == k)
                    def _():
                        act(
                            pltpu.make_async_copy(
                                r.at[pl.ds(span * NT, NT)],
                                out.at[pl.ds((span * K_NB + j) * NT, NT)],
                                sems.at[span * K_NB + j],
                            )
                        )

    each(lambda c: c.start())
    each(lambda c: c.wait())


def compact(idx, received, others):
    rows, cols = received[0].shape
    return pl.pallas_call(
        compact_kernel,
        out_shape=sds((K_NB * rows, cols)),
        in_specs=[SMEM] + [ANY] * 6,
        out_specs=ANY,
        scratch_shapes=[pltpu.SemaphoreType.DMA((4,))],
        compiler_params=params(1),
        cost_estimate=cost(1 * 10**9, 1024),
        name="compact",
    )(idx, *received, *others)


def source_columns(k, width):
    col = (lax.axis_index("mp") - k + N_MP) % N_MP
    return pl.ds(pl.multiple_of(col * width, width), width)


def attention(blocks):
    scores = [dot_t(q, k) for q, k, _ in blocks]
    tops = [jnp.max(s, axis=-1, keepdims=True) for s in scores]
    weights = [jnp.exp2((s - m) * EXP2_SCALE) for s, m in zip(scores, tops)]
    mixes = [dot(p.astype(BF), v) for p, (_, _, v) in zip(weights, blocks)]
    totals = [jnp.sum(p, axis=-1, keepdims=True) for p in weights]
    return [mix / total for mix, total in zip(mixes, totals)]


def encode_kernel(x0, x1, x2, x3, wq, wk, wv, first, second, src_out, src, sems):
    width = x0.shape[1]
    pairs = [(x, src.at[:, source_columns(k, width)]) for k, x in enumerate((x0, x1, x2, x3))]
    for c in run_copies(pairs, sems):
        c.wait()
    kept = pltpu.make_async_copy(src, src_out, sems.at[0])
    kept.start()
    source = src[...]
    q, k, v = (dot(source, w[...]).astype(BF) for w in (wq, wk, wv))
    places = [
        (slice(n * NT, (n + 1) * NT), slice(h * HEAD_DIM, (h + 1) * HEAD_DIM))
        for n in range(src.shape[0] // NT)
        for h in range(width // HEAD_DIM)
    ]
    for at, mix in zip(places, attention([(q[at], k[at], v[at]) for at in places])):
        rows, cols = at
        out = (first, second)[rows.start // (K_NB * NT)]
        begin = rows.start % (K_NB * NT)
        out[begin : begin + NT, cols] = mix.astype(BF)
    kept.wait()


def encode(pieces, wq, wk, wv):
    rows, width = pieces[0].shape
    depth = wq.shape[0]
    return pl.pallas_call(
        encode_kernel,
        out_shape=[sds((rows // 2, width))] * 2 + [pltpu.HBM((rows, depth), BF)],
        in_specs=[ANY] * 4 + [VMEM] * 3,
        out_specs=[VMEM, VMEM, ANY],
        scratch_shapes=[pltpu.VMEM((rows, depth), BF), pltpu.SemaphoreType.DMA((4,))],
        compiler_params=params(12),
        cost_estimate=cost(30 * 10**9, 1024),
        name="encode",
    )(*pieces, wq, wk, wv)


def load_kernel(w0, w_near, w_half, s_near, s_half, tie, wo_out, sems):
    width = w0.shape[0]
    half = width // 2
    core = lax.axis_index("seq") % 2
    begins = [(w0, 0), (w_near, (1 + 2 * core) * width), (s_near, (3 - 2 * core) * width)]
    begins += [(w_half, 2 * width + core * half), (s_half, 2 * width + (1 - core) * half)]
    pairs = []
    for w, begin in begins:
        rows = w.shape[0]
        pairs.append((w, wo_out.at[pl.ds(pl.multiple_of(begin, half), rows)]))
    for c in run_copies(pairs, sems):
        c.wait()


def load(wo, tie):
    depth = wo[0].shape[1]
    return pl.pallas_call(
        load_kernel,
        out_shape=pltpu.VMEM((depth, depth), BF),
        in_specs=[ANY] * 6,
        out_specs=ANY,
        scratch_shapes=[pltpu.SemaphoreType.DMA((5,))],
        compiler_params=params(1),
        cost_estimate=cost(3 * 10**9, 1024),
        name="load",
    )(*map(in_hbm, wo[:3]), *wo[3:], tie)


def cross_kernel(which, counts, src, a0, a1, a2, a3, wo, wk, wv, cq, so, out, src_s, attn, sems):
    nbrs, width = a0.shape
    pairs = [(a, attn.at[:, pl.ds(k * width, width)]) for k, a in enumerate((a0, a1, a2, a3))]
    copies = run_copies(pairs + [(src.at[pl.ds(which * nbrs, nbrs)], src_s)], sems)
    seq = lax.axis_index("seq")
    count = counts[0, seq * 2 + which]
    shape = (SPAN, nbrs)
    alive = lax.broadcasted_iota(jnp.int32, shape, 1) < count * NT
    if which == 1:
        past = (lax.broadcasted_iota(jnp.int32, shape, 0) > 0) & (seq == lax.axis_size("seq") - 1)
        alive = alive & jnp.logical_not(past)
    for c in copies[:4]:
        c.wait()
    mixed = dot(attn[...], wo[...])
    copies[4].wait()
    encoded = (src_s[...].astype(F32) + mixed).astype(BF)
    keys = dot(encoded, wk[...]).astype(BF)
    values = dot(encoded, wv[...]).astype(BF)
    rows = slice(which * SPAN, (which + 1) * SPAN)
    heads = [slice(h * HEAD_DIM, (h + 1) * HEAD_DIM) for h in range(cq.shape[1] // HEAD_DIM)]
    scores = [jnp.where(alive, dot_t(cq[rows, c], keys[:, c]), NEG_BIG) for c in heads]
    tops = [jnp.max(s, axis=-1, keepdims=True) for s in scores]
    weights = [jnp.exp2((s - m) * EXP2_SCALE) for s, m in zip(scores, tops)]
    weights = [jnp.where(alive, p, 0.0) for p in weights]
    mixes = [dot(p.astype(BF), values[:, c]) for p, c in zip(weights, heads)]
    totals = [jnp.sum(p, axis=-1, keepdims=True) for p in weights]
    for c, mix, total in zip(heads, mixes, totals):
        out[:, c] = (so[rows, c].astype(F32) + mix / jnp.maximum(total, 1.0)).astype(BF)


def cross(which, counts, source, attn, wo, wk, wv, cq, so):
    rows, depth = source.shape
    cols = cq.shape[1]

    def body(*refs):
        cross_kernel(which, *refs)

    return pl.pallas_call(
        body,
        out_shape=sds((SPAN, cols)),
        in_specs=[SMEM] + [ANY] * 5 + [VMEM] * 5,
        out_specs=VMEM,
        scratch_shapes=[
            pltpu.VMEM((rows // 2, depth), BF),
            pltpu.VMEM((rows // 2, depth), BF),
            pltpu.SemaphoreType.DMA((5,)),
        ],
        compiler_params=params(12),
        cost_estimate=cost(5 * 10**9, 1024),
        name="cross",
    )(counts, in_hbm(source), *attn, wo, wk, wv, cq, so)


def pack_kernel(q, k, v, wo, nbr_rows, nbr_owner, out, idx, half, rows, at_row, at_owner, sems):
    tok = q.shape[1]
    places = run_copies([(nbr_rows, at_row), (nbr_owner, at_owner)], sems)
    pairs = [(ref.at[0], rows.at[n]) for n, ref in enumerate((q, k, v))]
    count = half.shape[0]
    core = lax.axis_index("seq") % 2
    pairs.append((wo.at[pl.ds(pl.multiple_of(core * count, count), count)], half))
    copies = run_copies(pairs, sems.at[pl.ds(2, 4)])
    for c in places:
        c.wait()
    for span in range(2):
        for j in range(K_NB):
            idx[span * K_NB + j] = at_owner[0, span, j] * DB + at_row[0, span, j]
    for n, c in enumerate(copies[:3]):
        c.wait()
        for head in range(N_Z):
            cols = slice(head * HEAD_DIM, (head + 1) * HEAD_DIM)
            out[turned(head), n * tok : (n + 1) * tok, :] = rows[n, :, cols]
    copies[3].wait()


def pack(q, k, v, wo, nbr_rows, nbr_owner):
    _, tok, cols = q.shape
    return pl.pallas_call(
        pack_kernel,
        out_shape=[
            sds((N_Z, 3 * tok, HEAD_DIM)),
            sds((2 * K_NB,), jnp.int32),
            sds((wo.shape[0] // 2, wo.shape[1])),
        ],
        in_specs=[ANY] * 6,
        out_specs=[VMEM, SMEM, VMEM],
        scratch_shapes=[
            pltpu.VMEM((3, tok, cols), BF),
            pltpu.SMEM(nbr_rows.shape, jnp.int32),
            pltpu.SMEM(nbr_owner.shape, jnp.int32),
            pltpu.SemaphoreType.DMA((6,)),
        ],
        compiler_params=params(4),
        cost_estimate=cost(10**9, 1024),
        name="pack",
    )(*map(in_hbm, (q, k, v, wo, nbr_rows, nbr_owner)))


def attend_kernel(own, other, out):
    core = lax.axis_index("seq") % 2
    tok = out.shape[1]
    tokens = 2 * N_Z * tok

    def rows_of(ref, n, kind):
        at = slice(kind * tok, (kind + 1) * tok)
        rows = ref[1 : n + 1, at].reshape(-1, HEAD_DIM)
        return rows if n < N_Z else jnp.concatenate([rows, ref[0, at]], axis=0)

    def block_parts(z):
        here, after_z = turned(z), turned(turned(z))
        nxt = jnp.where(core == 0, other[here, :SPAN].astype(F32), other[after_z, :SPAN].astype(F32))
        both = jnp.concatenate([own[here, :tok].astype(F32), nxt], axis=0)
        rolled = pltpu.roll(both, both.shape[0] - (SPAN - 1), 0)[:tok].astype(BF)
        pos = (2 * z + core) * tok + SPAN - 1 + lax.broadcasted_iota(jnp.int32, (tok, 1), 0)
        pos = jnp.where(pos >= tokens, pos - tokens, pos)
        col = lax.broadcasted_iota(jnp.int32, (1, tok), 1)
        parts, values = [], []
        for n, ref, parity in ((z + 1, own, core), (min(z + 2, N_Z), other, 1 - core)):
            s = dot_t(rolled, rows_of(ref, n, 1))
            values.append(rows_of(ref, n, 2))
            for b in range(n):
                piece = s[:, b * tok : (b + 1) * tok]
                if b >= z or z == N_Z - 1:
                    piece = jnp.where((2 * b + parity) * tok + col <= pos, piece, NEG_BIG)
                parts.append(piece)
        return parts, values

    for group in ((0, 7, 3, 4), (1, 6, 2, 5)):
        made = [block_parts(z) for z in group]
        tops = [jnp.max(functools.reduce(jnp.maximum, parts), axis=-1, keepdims=True) for parts, _ in made]
        weights = [[jnp.exp2((s - m) * EXP2_SCALE) for s in parts] for (parts, _), m in zip(made, tops)]
        totals = [jnp.sum(functools.reduce(jnp.add, ps), axis=-1, keepdims=True) for ps in weights]
        mixes = []
        for ps, (_, (mine, theirs)) in zip(weights, made):
            p = jnp.concatenate([part.astype(BF) for part in ps], axis=1)
            split = mine.shape[0]
            mixes.append(dot(p[:, :split], mine) + dot(p[:, split:], theirs))
        for z, mix, total in zip(group, mixes, totals):
            out[turned(z)] = (mix / total).astype(BF)


def attend(own, other):
    tok = own.shape[1] // 3
    total = N_Z * tok
    return pl.pallas_call(
        attend_kernel,
        out_shape=sds((N_Z, tok, HEAD_DIM)),
        in_specs=[VMEM] * 2,
        out_specs=VMEM,
        compiler_params=params(12),
        cost_estimate=cost(10 * 10**9, 1024),
        name="attend",
    )(own, other)


def query_kernel(heads, wq, so, cq):
    for h in range(N_Z):
        cols = slice(h * HEAD_DIM, (h + 1) * HEAD_DIM)
        value = heads[turned(h)]
        so[:, cols] = value
        cq[:, cols] = dot(value, wq[h]).astype(BF)


def cross_queries(heads, wq):
    tok = heads.shape[1]
    cols = N_Z * HEAD_DIM
    return pl.pallas_call(
        query_kernel,
        out_shape=[sds((tok, cols))] * 2,
        in_specs=[VMEM] * 2,
        out_specs=[VMEM] * 2,
        compiler_params=params(4),
        cost_estimate=cost(1 * 10**9, 1024),
        name="cross_queries",
    )(heads, wq)


def place_kernel(received, first, second, out):
    rows = jnp.concatenate([received[...], first[...], second[...]], axis=0).astype(F32)
    out[0] = pltpu.roll(rows, rows.shape[0] - 1, 0)[: out.shape[1]].astype(BF)


def place(received, first, second):
    cols = first.shape[1]
    return pl.pallas_call(
        place_kernel,
        out_shape=sds((1, 2 * SPAN, cols)),
        in_specs=[VMEM] * 3,
        out_specs=VMEM,
        compiler_params=params(4),
        cost_estimate=cost(1 * 10**9, 1024),
        name="place",
    )(received, first, second)


def per_device(
    queries, keys_in, values_in, memory, enc_wq, enc_wk, enc_wv, enc_wo,
    cross_wk, cross_wv, cross_wq, nbr_rows, nbr_owner, nbr_count,
):
    packed, idx, wo_half = pack(queries, keys_in, values_in, enc_wo, nbr_rows, nbr_owner)
    packed = over_z(packed)
    asked = [idx] + [shifted(idx, "enc", k) for k in range(1, N_ENC)]
    near, far = to_sides(enc_wo), shifted(wo_half, "mp", 2)

    sent = fetch(asked, memory)
    received = [sent[0]] + [shifted(sent[k], "enc", -k) for k in range(1, N_ENC)]
    mine = compact(idx, received, (near, far))
    pieces = [mine] + [shifted(mine, "mp", k) for k in range(1, N_MP)]

    packed = after(packed, mine)
    heads = over_z(attend(packed, core_swap(packed)))
    so, cq = cross_queries(heads, cross_wq)

    early, late, source = encode(pieces, enc_wq, enc_wk, enc_wv)
    late = [late] + [shifted(late, "mp", k) for k in range(1, N_MP)]
    wo = load((enc_wo, near, far, core_swap(near), core_swap(far)), cq)
    early = after(early, wo)
    early = [early] + [shifted(early, "mp", k) for k in range(1, N_MP)]
    second = cross(1, nbr_count, source, late, wo, cross_wk, cross_wv, cq, so)
    passed = shifted(second, "seq", 1)
    first = cross(0, nbr_count, source, early, wo, cross_wk, cross_wv, cq, so)
    return place(passed, first, second)


def solution(mesh):
    return jax.shard_map(
        per_device,
        mesh=mesh,
        in_specs=(
            P("enc", "seq", "mp"),
            P("enc", "seq", "mp"),
            P("enc", "seq", "mp"),
            P("enc", None, "mp"),
            P(None, "mp"),
            P(None, "mp"),
            P(None, "mp"),
            P("mp", None),
            P(None, "mp"),
            P(None, "mp"),
            P("mp", None, None),
            P("enc", "seq", None),
            P("enc", "seq", None),
            P("enc", None),
        ),
        out_specs=P("enc", "seq", "mp"),
        check_vma=False,
    )
```

```python
import functools
import math

import jax
import jax.numpy as jnp
from jax import lax
from jax.experimental import pallas as pl
from jax.experimental.pallas import tpu as pltpu
from jax.sharding import PartitionSpec as P

HEAD_DIM = 128
SPAN = 64
K_NB = 2
NT = 128
DB = 32
N_ENC = 4
N_MP = 4
N_Z = 8
NEG_BIG = -1e30
SCALE = 1.0 / math.sqrt(HEAD_DIM)
EXP2_SCALE = SCALE * math.log2(math.e)
BF = jnp.bfloat16
F32 = jnp.float32

ANY = pl.BlockSpec(memory_space=pl.ANY)
SMEM = pl.BlockSpec(memory_space=pltpu.SMEM)
VMEM = pl.BlockSpec(memory_space=pltpu.VMEM)
MB = 1024 * 1024


def shifted(block, axis, distance):
    size = lax.axis_size(axis)
    return lax.ppermute(block, axis, [(i, (i + distance) % size) for i in range(size)])


def to_sides(block):
    seqs, mps = lax.axis_size("seq"), lax.axis_size("mp")
    route = [
        (s * mps + m, s * mps + (m + (1 if s % 2 == 0 else -1)) % mps)
        for s in range(seqs)
        for m in range(mps)
    ]
    return lax.ppermute(block, ("seq", "mp"), route)


def core_swap(block):
    size = lax.axis_size("seq")
    return lax.ppermute(block, "seq", [(i, i ^ 1) for i in range(size)])


def turned(z):
    return (z + 1) % N_Z


def over_z(blocks):
    groups = [[2 * (n - 1) % (2 * N_Z) + core for n in range(N_Z)] for core in range(2)]
    return lax.all_to_all(blocks, "seq", 0, 0, axis_index_groups=groups, tiled=True)


def in_hbm(x):
    return pltpu.with_memory_space_constraint(x, pltpu.HBM)


def after(x, *others):
    def kernel(*refs):
        pass

    return pl.pallas_call(
        kernel,
        out_shape=sds(x.shape, x.dtype),
        in_specs=[ANY] * (1 + len(others)),
        out_specs=ANY,
        input_output_aliases={0: 0},
        compiler_params=params(1),
        cost_estimate=cost(0, 1024),
        name="after",
    )(x, *others)


def sds(shape, dtype=BF):
    return jax.ShapeDtypeStruct(shape, dtype)


def params(limit_mb):
    return pltpu.CompilerParams(vmem_limit_bytes=limit_mb * MB)


def cost(flops, nbytes, trans=0):
    return pl.CostEstimate(flops=flops, bytes_accessed=nbytes, transcendentals=trans)


def dot(a, b):
    return jnp.dot(a, b, preferred_element_type=F32)


def dot_t(a, b):
    return lax.dot_general(a, b, (((1,), (1,)), ((), ())), preferred_element_type=F32)


def run_copies(pairs, sems):
    copies = [pltpu.make_async_copy(s, d, sems.at[n]) for n, (s, d) in enumerate(pairs)]
    for c in copies:
        c.start()
    return copies


def fetch_kernel(idx0, idx1, idx2, idx3, memory, s0, s1, s2, s3, sems):
    me = lax.axis_index("enc")
    pairs = []
    for idx, out in ((idx0, s0), (idx1, s1), (idx2, s2), (idx3, s3)):
        for span in range(2):
            row = jnp.int32(0)
            for j in range(K_NB):
                flat = idx[span * K_NB + j]
                row = jnp.where(flat // DB == me, flat % DB, row)
            pairs.append((memory.at[row], out.at[pl.ds(span * NT, NT)]))
    for c in run_copies(pairs, sems):
        c.wait()


def fetch(idx, memory):
    cols = memory.shape[2]
    return pl.pallas_call(
        fetch_kernel,
        out_shape=[sds((2 * NT, cols))] * 4,
        in_specs=[SMEM] * 4 + [ANY],
        out_specs=[ANY] * 4,
        scratch_shapes=[pltpu.SemaphoreType.DMA((8,))],
        compiler_params=params(1),
        cost_estimate=cost(5 * 10**9, 1024),
        name="fetch",
    )(*idx, in_hbm(memory))


def compact_kernel(idx, r0, r1, r2, r3, w1, w2, out):
    me = lax.axis_index("enc")
    for span in range(2):
        for j in range(K_NB):
            at = (idx[span * K_NB + j] // DB - me + N_ENC) % N_ENC
            for k, r in enumerate((r0, r1, r2, r3)):

                @pl.when(at == k)
                def _():
                    begin = (span * K_NB + j) * NT
                    out[begin : begin + NT] = r[span * NT : (span + 1) * NT]


def compact(idx, received, others):
    rows, cols = received[0].shape
    return pl.pallas_call(
        compact_kernel,
        out_shape=sds((K_NB * rows, cols)),
        in_specs=[SMEM] + [VMEM] * 4 + [ANY] * 2,
        out_specs=VMEM,
        compiler_params=params(4),
        cost_estimate=cost(1 * 10**9, 1024),
        name="compact",
    )(idx, *received, *others)


def source_columns(k, width):
    col = (lax.axis_index("mp") - k + N_MP) % N_MP
    return pl.ds(pl.multiple_of(col * width, width), width)


def attention(blocks):
    scores = [dot_t(q, k) for q, k, _ in blocks]
    tops = [jnp.max(s, axis=-1, keepdims=True) for s in scores]
    weights = [jnp.exp2((s - m) * EXP2_SCALE) for s, m in zip(scores, tops)]
    mixes = [dot(p.astype(BF), v) for p, (_, _, v) in zip(weights, blocks)]
    totals = [jnp.sum(p, axis=-1, keepdims=True) for p in weights]
    return [mix / total for mix, total in zip(mixes, totals)]


def encode_kernel(x0, x1, x2, x3, wq, wk, wv, first, second, src_out, src, sems):
    width = x0.shape[1]
    pairs = [(x, src.at[:, source_columns(k, width)]) for k, x in enumerate((x0, x1, x2, x3))]
    for c in run_copies(pairs, sems):
        c.wait()
    kept = pltpu.make_async_copy(src, src_out, sems.at[0])
    kept.start()
    source = src[...]
    q, k, v = (dot(source, w[...]).astype(BF) for w in (wq, wk, wv))
    places = [
        (slice(n * NT, (n + 1) * NT), slice(h * HEAD_DIM, (h + 1) * HEAD_DIM))
        for n in range(src.shape[0] // NT)
        for h in range(width // HEAD_DIM)
    ]
    for at, mix in zip(places, attention([(q[at], k[at], v[at]) for at in places])):
        rows, cols = at
        out = (first, second)[rows.start // (K_NB * NT)]
        begin = rows.start % (K_NB * NT)
        out[begin : begin + NT, cols] = mix.astype(BF)
    kept.wait()


def encode(pieces, wq, wk, wv):
    rows, width = pieces[0].shape
    depth = wq.shape[0]
    return pl.pallas_call(
        encode_kernel,
        out_shape=[sds((rows // 2, width))] * 2 + [pltpu.HBM((rows, depth), BF)],
        in_specs=[ANY] * 4 + [VMEM] * 3,
        out_specs=[VMEM, VMEM, ANY],
        scratch_shapes=[pltpu.VMEM((rows, depth), BF), pltpu.SemaphoreType.DMA((4,))],
        compiler_params=params(12),
        cost_estimate=cost(30 * 10**9, 1024),
        name="encode",
    )(*pieces, wq, wk, wv)


def load_kernel(w0, w_near, w_half, s_near, s_half, heads, wq, wo_out, so, cq, sems):
    width = w0.shape[0]
    half = width // 2
    core = lax.axis_index("seq") % 2
    begins = [(w0, 0), (w_near, (1 + 2 * core) * width), (s_near, (3 - 2 * core) * width)]
    begins += [(w_half, 2 * width + core * half), (s_half, 2 * width + (1 - core) * half)]
    pairs = []
    for w, begin in begins:
        rows = w.shape[0]
        pairs.append((w, wo_out.at[pl.ds(pl.multiple_of(begin, half), rows)]))
    copies = run_copies(pairs, sems)
    for h in range(N_Z):
        cols = slice(h * HEAD_DIM, (h + 1) * HEAD_DIM)
        value = heads[turned(h)]
        so[:, cols] = value
        cq[:, cols] = dot(value, wq[h]).astype(BF)
    for c in copies:
        c.wait()


def load(wo, heads, wq):
    depth = wo[0].shape[1]
    tok, cols = heads.shape[1], N_Z * HEAD_DIM
    return pl.pallas_call(
        load_kernel,
        out_shape=[pltpu.VMEM((depth, depth), BF), sds((tok, cols)), sds((tok, cols))],
        in_specs=[ANY] * 5 + [VMEM] * 2,
        out_specs=[ANY, VMEM, VMEM],
        scratch_shapes=[pltpu.SemaphoreType.DMA((5,))],
        compiler_params=params(4),
        cost_estimate=cost(3 * 10**9, 1024),
        name="load",
    )(*map(in_hbm, wo[:3]), *wo[3:], heads, wq)


def cross_kernel(which, counts, src, a0, a1, a2, a3, wo, wk, wv, cq, so, out, src_s, attn, sems):
    nbrs, width = a0.shape
    pairs = [(a, attn.at[:, pl.ds(k * width, width)]) for k, a in enumerate((a0, a1, a2, a3))]
    copies = run_copies(pairs + [(src.at[pl.ds(which * nbrs, nbrs)], src_s)], sems)
    seq = lax.axis_index("seq")
    count = counts[0, seq * 2 + which]
    shape = (SPAN, nbrs)
    alive = lax.broadcasted_iota(jnp.int32, shape, 1) < count * NT
    if which == 1:
        past = (lax.broadcasted_iota(jnp.int32, shape, 0) > 0) & (seq == lax.axis_size("seq") - 1)
        alive = alive & jnp.logical_not(past)
    for c in copies[:4]:
        c.wait()
    mixed = dot(attn[...], wo[...])
    copies[4].wait()
    encoded = (src_s[...].astype(F32) + mixed).astype(BF)
    keys = dot(encoded, wk[...]).astype(BF)
    values = dot(encoded, wv[...]).astype(BF)
    rows = slice(which * SPAN, (which + 1) * SPAN)
    heads = [slice(h * HEAD_DIM, (h + 1) * HEAD_DIM) for h in range(cq.shape[1] // HEAD_DIM)]
    scores = [jnp.where(alive, dot_t(cq[rows, c], keys[:, c]), NEG_BIG) for c in heads]
    tops = [jnp.max(s, axis=-1, keepdims=True) for s in scores]
    weights = [jnp.exp2((s - m) * EXP2_SCALE) for s, m in zip(scores, tops)]
    weights = [jnp.where(alive, p, 0.0) for p in weights]
    mixes = [dot(p.astype(BF), values[:, c]) for p, c in zip(weights, heads)]
    totals = [jnp.sum(p, axis=-1, keepdims=True) for p in weights]
    for c, mix, total in zip(heads, mixes, totals):
        out[:, c] = (so[rows, c].astype(F32) + mix / jnp.maximum(total, 1.0)).astype(BF)


def cross(which, counts, source, attn, wo, wk, wv, cq, so):
    rows, depth = source.shape
    cols = cq.shape[1]

    def body(*refs):
        cross_kernel(which, *refs)

    return pl.pallas_call(
        body,
        out_shape=sds((SPAN, cols)),
        in_specs=[SMEM] + [ANY] * 5 + [VMEM] * 5,
        out_specs=VMEM,
        scratch_shapes=[
            pltpu.VMEM((rows // 2, depth), BF),
            pltpu.VMEM((rows // 2, depth), BF),
            pltpu.SemaphoreType.DMA((5,)),
        ],
        compiler_params=params(12),
        cost_estimate=cost(5 * 10**9, 1024),
        name="cross",
    )(counts, in_hbm(source), *attn, wo, wk, wv, cq, so)


def pack_kernel(q, k, v, wo, nbr_rows, nbr_owner, out, idx, half, rows, at_row, at_owner, sems):
    tok = q.shape[1]
    places = run_copies([(nbr_rows, at_row), (nbr_owner, at_owner)], sems)
    pairs = [(ref.at[0], rows.at[n]) for n, ref in enumerate((q, k, v))]
    count = half.shape[0]
    core = lax.axis_index("seq") % 2
    pairs.append((wo.at[pl.ds(pl.multiple_of(core * count, count), count)], half))
    copies = run_copies(pairs, sems.at[pl.ds(2, 4)])
    for c in places:
        c.wait()
    for span in range(2):
        for j in range(K_NB):
            idx[span * K_NB + j] = at_owner[0, span, j] * DB + at_row[0, span, j]
    for n, c in enumerate(copies[:3]):
        c.wait()
        for head in range(N_Z):
            cols = slice(head * HEAD_DIM, (head + 1) * HEAD_DIM)
            out[turned(head), n * tok : (n + 1) * tok, :] = rows[n, :, cols]
    copies[3].wait()


def pack(q, k, v, wo, nbr_rows, nbr_owner):
    _, tok, cols = q.shape
    return pl.pallas_call(
        pack_kernel,
        out_shape=[
            sds((N_Z, 3 * tok, HEAD_DIM)),
            sds((2 * K_NB,), jnp.int32),
            sds((wo.shape[0] // 2, wo.shape[1])),
        ],
        in_specs=[ANY] * 6,
        out_specs=[VMEM, SMEM, VMEM],
        scratch_shapes=[
            pltpu.VMEM((3, tok, cols), BF),
            pltpu.SMEM(nbr_rows.shape, jnp.int32),
            pltpu.SMEM(nbr_owner.shape, jnp.int32),
            pltpu.SemaphoreType.DMA((6,)),
        ],
        compiler_params=params(4),
        cost_estimate=cost(10**9, 1024),
        name="pack",
    )(*map(in_hbm, (q, k, v, wo, nbr_rows, nbr_owner)))


def attend_kernel(own, other, out):
    core = lax.axis_index("seq") % 2
    tok = out.shape[1]
    tokens = 2 * N_Z * tok

    def rows_of(ref, n, kind):
        at = slice(kind * tok, (kind + 1) * tok)
        rows = ref[1 : n + 1, at].reshape(-1, HEAD_DIM)
        return rows if n < N_Z else jnp.concatenate([rows, ref[0, at]], axis=0)

    def block_parts(z):
        here, after_z = turned(z), turned(turned(z))
        nxt = jnp.where(core == 0, other[here, :SPAN].astype(F32), other[after_z, :SPAN].astype(F32))
        both = jnp.concatenate([own[here, :tok].astype(F32), nxt], axis=0)
        rolled = pltpu.roll(both, both.shape[0] - (SPAN - 1), 0)[:tok].astype(BF)
        pos = (2 * z + core) * tok + SPAN - 1 + lax.broadcasted_iota(jnp.int32, (tok, 1), 0)
        pos = jnp.where(pos >= tokens, pos - tokens, pos)
        col = lax.broadcasted_iota(jnp.int32, (1, tok), 1)
        parts, values = [], []
        for n, ref, parity in ((z + 1, own, core), (min(z + 2, N_Z), other, 1 - core)):
            s = dot_t(rolled, rows_of(ref, n, 1))
            values.append(rows_of(ref, n, 2))
            for b in range(n):
                piece = s[:, b * tok : (b + 1) * tok]
                if b >= z or z == N_Z - 1:
                    piece = jnp.where((2 * b + parity) * tok + col <= pos, piece, NEG_BIG)
                parts.append(piece)
        return parts, values

    for group in ((0, 7, 3, 4), (1, 6, 2, 5)):
        made = [block_parts(z) for z in group]
        tops = [jnp.max(functools.reduce(jnp.maximum, parts), axis=-1, keepdims=True) for parts, _ in made]
        weights = [[jnp.exp2((s - m) * EXP2_SCALE) for s in parts] for (parts, _), m in zip(made, tops)]
        totals = [jnp.sum(functools.reduce(jnp.add, ps), axis=-1, keepdims=True) for ps in weights]
        mixes = []
        for ps, (_, (mine, theirs)) in zip(weights, made):
            p = jnp.concatenate([part.astype(BF) for part in ps], axis=1)
            split = mine.shape[0]
            mixes.append(dot(p[:, :split], mine) + dot(p[:, split:], theirs))
        for z, mix, total in zip(group, mixes, totals):
            out[turned(z)] = (mix / total).astype(BF)


def attend(own, other):
    tok = own.shape[1] // 3
    total = N_Z * tok
    return pl.pallas_call(
        attend_kernel,
        out_shape=sds((N_Z, tok, HEAD_DIM)),
        in_specs=[VMEM] * 2,
        out_specs=VMEM,
        compiler_params=params(12),
        cost_estimate=cost(10 * 10**9, 1024),
        name="attend",
    )(own, other)


def place_kernel(received, first, second, out):
    rows = jnp.concatenate([received[...], first[...], second[...]], axis=0).astype(F32)
    out[0] = pltpu.roll(rows, rows.shape[0] - 1, 0)[: out.shape[1]].astype(BF)


def place(received, first, second):
    cols = first.shape[1]
    return pl.pallas_call(
        place_kernel,
        out_shape=sds((1, 2 * SPAN, cols)),
        in_specs=[VMEM] * 3,
        out_specs=VMEM,
        compiler_params=params(4),
        cost_estimate=cost(1 * 10**9, 1024),
        name="place",
    )(received, first, second)


def per_device(
    queries, keys_in, values_in, memory, enc_wq, enc_wk, enc_wv, enc_wo,
    cross_wk, cross_wv, cross_wq, nbr_rows, nbr_owner, nbr_count,
):
    packed, idx, wo_half = pack(queries, keys_in, values_in, enc_wo, nbr_rows, nbr_owner)
    packed = over_z(packed)
    asked = [idx] + [shifted(idx, "enc", k) for k in range(1, N_ENC)]
    near, far = to_sides(enc_wo), shifted(wo_half, "mp", 2)

    sent = fetch(asked, memory)
    received = [sent[0]] + [shifted(sent[k], "enc", -k) for k in range(1, N_ENC)]
    mine = compact(idx, received, (near, far))
    pieces = [mine] + [shifted(mine, "mp", k) for k in range(1, N_MP)]

    packed = after(packed, mine)
    heads = over_z(attend(packed, core_swap(packed)))

    early, late, source = encode(pieces, enc_wq, enc_wk, enc_wv)
    late = [late] + [shifted(late, "mp", k) for k in range(1, N_MP)]
    wo, so, cq = load((enc_wo, near, far, core_swap(near), core_swap(far)), heads, cross_wq)
    early = after(early, wo)
    early = [early] + [shifted(early, "mp", k) for k in range(1, N_MP)]
    second = cross(1, nbr_count, source, late, wo, cross_wk, cross_wv, cq, so)
    passed = shifted(second, "seq", 1)
    first = cross(0, nbr_count, source, early, wo, cross_wk, cross_wv, cq, so)
    return place(passed, first, second)


def solution(mesh):
    return jax.shard_map(
        per_device,
        mesh=mesh,
        in_specs=(
            P("enc", "seq", "mp"),
            P("enc", "seq", "mp"),
            P("enc", "seq", "mp"),
            P("enc", None, "mp"),
            P(None, "mp"),
            P(None, "mp"),
            P(None, "mp"),
            P("mp", None),
            P(None, "mp"),
            P(None, "mp"),
            P("mp", None, None),
            P("enc", "seq", None),
            P("enc", "seq", None),
            P("enc", None),
        ),
        out_specs=P("enc", "seq", "mp"),
        check_vma=False,
    )
```

```python
import functools
import math

import jax
import jax.numpy as jnp
from jax import lax
from jax.experimental import pallas as pl
from jax.experimental.pallas import tpu as pltpu
from jax.sharding import PartitionSpec as P

HEAD_DIM = 128
SPAN = 64
K_NB = 2
NT = 128
DB = 32
N_ENC = 4
N_MP = 4
N_Z = 8
NEG_BIG = -1e30
SCALE = 1.0 / math.sqrt(HEAD_DIM)
EXP2_SCALE = SCALE * math.log2(math.e)
BF = jnp.bfloat16
F32 = jnp.float32

ANY = pl.BlockSpec(memory_space=pl.ANY)
SMEM = pl.BlockSpec(memory_space=pltpu.SMEM)
VMEM = pl.BlockSpec(memory_space=pltpu.VMEM)
MB = 1024 * 1024


def shifted(block, axis, distance):
    size = lax.axis_size(axis)
    return lax.ppermute(block, axis, [(i, (i + distance) % size) for i in range(size)])


def to_sides(block):
    seqs, mps = lax.axis_size("seq"), lax.axis_size("mp")
    route = [
        (s * mps + m, s * mps + (m + (1 if s % 2 == 0 else -1)) % mps)
        for s in range(seqs)
        for m in range(mps)
    ]
    return lax.ppermute(block, ("seq", "mp"), route)


def core_swap(block):
    size = lax.axis_size("seq")
    return lax.ppermute(block, "seq", [(i, i ^ 1) for i in range(size)])


def turned(z):
    return (z + 1) % N_Z


def over_z(blocks):
    groups = [[2 * (n - 1) % (2 * N_Z) + core for n in range(N_Z)] for core in range(2)]
    return lax.all_to_all(blocks, "seq", 0, 0, axis_index_groups=groups, tiled=True)


def in_hbm(x):
    return pltpu.with_memory_space_constraint(x, pltpu.HBM)


def after(x, *others):
    def kernel(*refs):
        pass

    return pl.pallas_call(
        kernel,
        out_shape=sds(x.shape, x.dtype),
        in_specs=[ANY] * (1 + len(others)),
        out_specs=ANY,
        input_output_aliases={0: 0},
        compiler_params=params(1),
        cost_estimate=cost(0, 1024),
        name="after",
    )(x, *others)


def sds(shape, dtype=BF):
    return jax.ShapeDtypeStruct(shape, dtype)


def params(limit_mb):
    return pltpu.CompilerParams(vmem_limit_bytes=limit_mb * MB)


def cost(flops, nbytes, trans=0):
    return pl.CostEstimate(flops=flops, bytes_accessed=nbytes, transcendentals=trans)


def dot(a, b):
    return jnp.dot(a, b, preferred_element_type=F32)


def dot_t(a, b):
    return lax.dot_general(a, b, (((1,), (1,)), ((), ())), preferred_element_type=F32)


def run_copies(pairs, sems):
    copies = [pltpu.make_async_copy(s, d, sems.at[n]) for n, (s, d) in enumerate(pairs)]
    for c in copies:
        c.start()
    return copies


def fetch_kernel(idx0, idx1, idx2, idx3, memory, s0, s1, s2, s3, sems):
    me = lax.axis_index("enc")
    pairs = []
    for idx, out in ((idx0, s0), (idx1, s1), (idx2, s2), (idx3, s3)):
        for span in range(2):
            row = jnp.int32(0)
            for j in range(K_NB):
                flat = idx[span * K_NB + j]
                row = jnp.where(flat // DB == me, flat % DB, row)
            pairs.append((memory.at[row], out.at[pl.ds(span * NT, NT)]))
    for c in run_copies(pairs, sems):
        c.wait()


def fetch(idx, memory):
    cols = memory.shape[2]
    return pl.pallas_call(
        fetch_kernel,
        out_shape=[sds((2 * NT, cols))] * 4,
        in_specs=[SMEM] * 4 + [ANY],
        out_specs=[ANY] * 4,
        scratch_shapes=[pltpu.SemaphoreType.DMA((8,))],
        compiler_params=params(1),
        cost_estimate=cost(5 * 10**9, 1024),
        name="fetch",
    )(*idx, in_hbm(memory))


def compact_kernel(idx, r0, r1, r2, r3, out):
    me = lax.axis_index("enc")
    for span in range(2):
        for j in range(K_NB):
            at = (idx[span * K_NB + j] // DB - me + N_ENC) % N_ENC
            for k, r in enumerate((r0, r1, r2, r3)):

                @pl.when(at == k)
                def _():
                    begin = (span * K_NB + j) * NT
                    out[begin : begin + NT] = r[span * NT : (span + 1) * NT]


def compact(idx, received):
    rows, cols = received[0].shape
    return pl.pallas_call(
        compact_kernel,
        out_shape=sds((K_NB * rows, cols)),
        in_specs=[SMEM] + [VMEM] * 4,
        out_specs=VMEM,
        compiler_params=params(4),
        cost_estimate=cost(1 * 10**9, 1024),
        name="compact",
    )(idx, *received)


def source_columns(k, width):
    col = (lax.axis_index("mp") - k + N_MP) % N_MP
    return pl.ds(pl.multiple_of(col * width, width), width)


def attention(blocks):
    scores = [dot_t(q, k) for q, k, _ in blocks]
    tops = [jnp.max(s, axis=-1, keepdims=True) for s in scores]
    weights = [jnp.exp2((s - m) * EXP2_SCALE) for s, m in zip(scores, tops)]
    mixes = [dot(p.astype(BF), v) for p, (_, _, v) in zip(weights, blocks)]
    totals = [jnp.sum(p, axis=-1, keepdims=True) for p in weights]
    return [mix / total for mix, total in zip(mixes, totals)]


def encode_kernel(x0, x1, x2, x3, wq, wk, wv, first, second, src_out, src, sems):
    width = x0.shape[1]
    pairs = [(x, src.at[:, source_columns(k, width)]) for k, x in enumerate((x0, x1, x2, x3))]
    for c in run_copies(pairs, sems):
        c.wait()
    kept = pltpu.make_async_copy(src, src_out, sems.at[0])
    kept.start()
    source = src[...]
    q, k, v = (dot(source, w[...]).astype(BF) for w in (wq, wk, wv))
    places = [
        (slice(n * NT, (n + 1) * NT), slice(h * HEAD_DIM, (h + 1) * HEAD_DIM))
        for n in range(src.shape[0] // NT)
        for h in range(width // HEAD_DIM)
    ]
    for at, mix in zip(places, attention([(q[at], k[at], v[at]) for at in places])):
        rows, cols = at
        out = (first, second)[rows.start // (K_NB * NT)]
        begin = rows.start % (K_NB * NT)
        out[begin : begin + NT, cols] = mix.astype(BF)
    kept.wait()


def encode(pieces, wq, wk, wv):
    rows, width = pieces[0].shape
    depth = wq.shape[0]
    return pl.pallas_call(
        encode_kernel,
        out_shape=[sds((rows // 2, width))] * 2 + [pltpu.HBM((rows, depth), BF)],
        in_specs=[ANY] * 4 + [VMEM] * 3,
        out_specs=[VMEM, VMEM, ANY],
        scratch_shapes=[pltpu.VMEM((rows, depth), BF), pltpu.SemaphoreType.DMA((4,))],
        compiler_params=params(12),
        cost_estimate=cost(30 * 10**9, 1024),
        name="encode",
    )(*pieces, wq, wk, wv)


def load_kernel(w0, w_near, w_half, s_near, s_half, heads, wq, wo_out, so, cq, sems):
    width = w0.shape[0]
    half = width // 2
    core = lax.axis_index("seq") % 2
    begins = [(w0, 0), (w_near, (1 + 2 * core) * width), (s_near, (3 - 2 * core) * width)]
    begins += [(w_half, 2 * width + core * half), (s_half, 2 * width + (1 - core) * half)]
    pairs = []
    for w, begin in begins:
        rows = w.shape[0]
        pairs.append((w, wo_out.at[pl.ds(pl.multiple_of(begin, half), rows)]))
    copies = run_copies(pairs, sems)
    for h in range(N_Z):
        cols = slice(h * HEAD_DIM, (h + 1) * HEAD_DIM)
        value = heads[turned(h)]
        so[:, cols] = value
        cq[:, cols] = dot(value, wq[h]).astype(BF)
    for c in copies:
        c.wait()


def load(wo, heads, wq):
    depth = wo[0].shape[1]
    tok, cols = heads.shape[1], N_Z * HEAD_DIM
    return pl.pallas_call(
        load_kernel,
        out_shape=[pltpu.VMEM((depth, depth), BF), sds((tok, cols)), sds((tok, cols))],
        in_specs=[ANY] * 5 + [VMEM] * 2,
        out_specs=[ANY, VMEM, VMEM],
        scratch_shapes=[pltpu.SemaphoreType.DMA((5,))],
        compiler_params=params(4),
        cost_estimate=cost(3 * 10**9, 1024),
        name="load",
    )(*map(in_hbm, wo[:3]), *wo[3:], heads, wq)


def cross_kernel(which, counts, src, a0, a1, a2, a3, wo, wk, wv, cq, so, out, src_s, attn, sems):
    nbrs, width = a0.shape
    pairs = [(a, attn.at[:, pl.ds(k * width, width)]) for k, a in enumerate((a0, a1, a2, a3))]
    copies = run_copies(pairs + [(src.at[pl.ds(which * nbrs, nbrs)], src_s)], sems)
    seq = lax.axis_index("seq")
    count = counts[0, seq * 2 + which]
    shape = (SPAN, nbrs)
    alive = lax.broadcasted_iota(jnp.int32, shape, 1) < count * NT
    if which == 1:
        past = (lax.broadcasted_iota(jnp.int32, shape, 0) > 0) & (seq == lax.axis_size("seq") - 1)
        alive = alive & jnp.logical_not(past)
    for c in copies[:4]:
        c.wait()
    mixed = dot(attn[...], wo[...])
    copies[4].wait()
    encoded = (src_s[...].astype(F32) + mixed).astype(BF)
    keys = dot(encoded, wk[...]).astype(BF)
    values = dot(encoded, wv[...]).astype(BF)
    rows = slice(which * SPAN, (which + 1) * SPAN)
    heads = [slice(h * HEAD_DIM, (h + 1) * HEAD_DIM) for h in range(cq.shape[1] // HEAD_DIM)]
    scores = [jnp.where(alive, dot_t(cq[rows, c], keys[:, c]), NEG_BIG) for c in heads]
    tops = [jnp.max(s, axis=-1, keepdims=True) for s in scores]
    weights = [jnp.exp2((s - m) * EXP2_SCALE) for s, m in zip(scores, tops)]
    weights = [jnp.where(alive, p, 0.0) for p in weights]
    mixes = [dot(p.astype(BF), values[:, c]) for p, c in zip(weights, heads)]
    totals = [jnp.sum(p, axis=-1, keepdims=True) for p in weights]
    for c, mix, total in zip(heads, mixes, totals):
        out[:, c] = (so[rows, c].astype(F32) + mix / jnp.maximum(total, 1.0)).astype(BF)


def cross(which, counts, source, attn, wo, wk, wv, cq, so):
    rows, depth = source.shape
    cols = cq.shape[1]

    def body(*refs):
        cross_kernel(which, *refs)

    return pl.pallas_call(
        body,
        out_shape=sds((SPAN, cols)),
        in_specs=[SMEM] + [ANY] * 5 + [VMEM] * 5,
        out_specs=VMEM,
        scratch_shapes=[
            pltpu.VMEM((rows // 2, depth), BF),
            pltpu.VMEM((rows // 2, depth), BF),
            pltpu.SemaphoreType.DMA((5,)),
        ],
        compiler_params=params(12),
        cost_estimate=cost(5 * 10**9, 1024),
        name="cross",
    )(counts, in_hbm(source), *attn, wo, wk, wv, cq, so)


def pack_kernel(q, k, v, wo, nbr_rows, nbr_owner, out, idx, half, rows, at_row, at_owner, sems):
    tok = q.shape[1]
    places = run_copies([(nbr_rows, at_row), (nbr_owner, at_owner)], sems)
    pairs = [(ref.at[0], rows.at[n]) for n, ref in enumerate((q, k, v))]
    count = half.shape[0]
    core = lax.axis_index("seq") % 2
    pairs.append((wo.at[pl.ds(pl.multiple_of(core * count, count), count)], half))
    copies = run_copies(pairs, sems.at[pl.ds(2, 4)])
    for c in places:
        c.wait()
    for span in range(2):
        for j in range(K_NB):
            idx[span * K_NB + j] = at_owner[0, span, j] * DB + at_row[0, span, j]
    for n, c in enumerate(copies[:3]):
        c.wait()
        for head in range(N_Z):
            cols = slice(head * HEAD_DIM, (head + 1) * HEAD_DIM)
            out[turned(head), n * tok : (n + 1) * tok, :] = rows[n, :, cols]
    copies[3].wait()


def pack(q, k, v, wo, nbr_rows, nbr_owner):
    _, tok, cols = q.shape
    return pl.pallas_call(
        pack_kernel,
        out_shape=[
            sds((N_Z, 3 * tok, HEAD_DIM)),
            sds((2 * K_NB,), jnp.int32),
            sds((wo.shape[0] // 2, wo.shape[1])),
        ],
        in_specs=[ANY] * 6,
        out_specs=[VMEM, SMEM, VMEM],
        scratch_shapes=[
            pltpu.VMEM((3, tok, cols), BF),
            pltpu.SMEM(nbr_rows.shape, jnp.int32),
            pltpu.SMEM(nbr_owner.shape, jnp.int32),
            pltpu.SemaphoreType.DMA((6,)),
        ],
        compiler_params=params(4),
        cost_estimate=cost(10**9, 1024),
        name="pack",
    )(*map(in_hbm, (q, k, v, wo, nbr_rows, nbr_owner)))


def attend_kernel(own, other, out):
    core = lax.axis_index("seq") % 2
    tok = out.shape[1]
    tokens = 2 * N_Z * tok

    def rows_of(ref, n, kind):
        at = slice(kind * tok, (kind + 1) * tok)
        rows = ref[1 : n + 1, at].reshape(-1, HEAD_DIM)
        return rows if n < N_Z else jnp.concatenate([rows, ref[0, at]], axis=0)

    def block_parts(z):
        here, after_z = turned(z), turned(turned(z))
        nxt = jnp.where(core == 0, other[here, :SPAN].astype(F32), other[after_z, :SPAN].astype(F32))
        both = jnp.concatenate([own[here, :tok].astype(F32), nxt], axis=0)
        rolled = pltpu.roll(both, both.shape[0] - (SPAN - 1), 0)[:tok].astype(BF)
        pos = (2 * z + core) * tok + SPAN - 1 + lax.broadcasted_iota(jnp.int32, (tok, 1), 0)
        pos = jnp.where(pos >= tokens, pos - tokens, pos)
        col = lax.broadcasted_iota(jnp.int32, (1, tok), 1)
        parts, values = [], []
        for n, ref, parity in ((z + 1, own, core), (min(z + 2, N_Z), other, 1 - core)):
            s = dot_t(rolled, rows_of(ref, n, 1))
            values.append(rows_of(ref, n, 2))
            for b in range(n):
                piece = s[:, b * tok : (b + 1) * tok]
                if b >= z or z == N_Z - 1:
                    piece = jnp.where((2 * b + parity) * tok + col <= pos, piece, NEG_BIG)
                parts.append(piece)
        return parts, values

    for group in ((0, 7, 3, 4), (1, 6, 2, 5)):
        made = [block_parts(z) for z in group]
        tops = [jnp.max(functools.reduce(jnp.maximum, parts), axis=-1, keepdims=True) for parts, _ in made]
        weights = [[jnp.exp2((s - m) * EXP2_SCALE) for s in parts] for (parts, _), m in zip(made, tops)]
        totals = [jnp.sum(functools.reduce(jnp.add, ps), axis=-1, keepdims=True) for ps in weights]
        mixes = []
        for ps, (_, (mine, theirs)) in zip(weights, made):
            p = jnp.concatenate([part.astype(BF) for part in ps], axis=1)
            split = mine.shape[0]
            mixes.append(dot(p[:, :split], mine) + dot(p[:, split:], theirs))
        for z, mix, total in zip(group, mixes, totals):
            out[turned(z)] = (mix / total).astype(BF)


def attend(own, other):
    tok = own.shape[1] // 3
    total = N_Z * tok
    return pl.pallas_call(
        attend_kernel,
        out_shape=sds((N_Z, tok, HEAD_DIM)),
        in_specs=[VMEM] * 2,
        out_specs=VMEM,
        compiler_params=params(12),
        cost_estimate=cost(10 * 10**9, 1024),
        name="attend",
    )(own, other)


def place_kernel(received, first, second, out):
    rows = jnp.concatenate([received[...], first[...], second[...]], axis=0).astype(F32)
    out[0] = pltpu.roll(rows, rows.shape[0] - 1, 0)[: out.shape[1]].astype(BF)


def place(received, first, second):
    cols = first.shape[1]
    return pl.pallas_call(
        place_kernel,
        out_shape=sds((1, 2 * SPAN, cols)),
        in_specs=[VMEM] * 3,
        out_specs=VMEM,
        compiler_params=params(4),
        cost_estimate=cost(1 * 10**9, 1024),
        name="place",
    )(received, first, second)


def per_device(
    queries, keys_in, values_in, memory, enc_wq, enc_wk, enc_wv, enc_wo,
    cross_wk, cross_wv, cross_wq, nbr_rows, nbr_owner, nbr_count,
):
    packed, idx, wo_half = pack(queries, keys_in, values_in, enc_wo, nbr_rows, nbr_owner)
    packed = over_z(packed)
    asked = [idx] + [shifted(idx, "enc", k) for k in range(1, N_ENC)]
    near, far = to_sides(enc_wo), shifted(wo_half, "mp", 2)

    sent = fetch(asked, memory)
    received = [sent[0]] + [shifted(sent[k], "enc", -k) for k in range(1, N_ENC)]
    mine = compact(idx, received)
    pieces = [mine] + [shifted(mine, "mp", k) for k in range(1, N_MP)]

    packed = after(packed, mine, near, far)
    heads = over_z(attend(packed, core_swap(packed)))

    early, late, source = encode(pieces, enc_wq, enc_wk, enc_wv)
    late = [late] + [shifted(late, "mp", k) for k in range(1, N_MP)]
    wo, so, cq = load((enc_wo, near, far, core_swap(near), core_swap(far)), heads, cross_wq)
    early = after(early, wo)
    early = [early] + [shifted(early, "mp", k) for k in range(1, N_MP)]
    second = cross(1, nbr_count, source, late, wo, cross_wk, cross_wv, cq, so)
    passed = shifted(second, "seq", 1)
    first = cross(0, nbr_count, source, early, wo, cross_wk, cross_wv, cq, so)
    return place(passed, first, second)


def solution(mesh):
    return jax.shard_map(
        per_device,
        mesh=mesh,
        in_specs=(
            P("enc", "seq", "mp"),
            P("enc", "seq", "mp"),
            P("enc", "seq", "mp"),
            P("enc", None, "mp"),
            P(None, "mp"),
            P(None, "mp"),
            P(None, "mp"),
            P("mp", None),
            P(None, "mp"),
            P(None, "mp"),
            P("mp", None, None),
            P("enc", "seq", None),
            P("enc", "seq", None),
            P("enc", None),
        ),
        out_specs=P("enc", "seq", "mp"),
        check_vma=False,
    )
```

```python
import functools
import math

import jax
import jax.numpy as jnp
from jax import lax
from jax.experimental import pallas as pl
from jax.experimental.pallas import tpu as pltpu
from jax.sharding import PartitionSpec as P

HEAD_DIM = 128
SPAN = 64
K_NB = 2
NT = 128
DB = 32
N_ENC = 4
N_MP = 4
N_Z = 8
NEG_BIG = -1e30
SCALE = 1.0 / math.sqrt(HEAD_DIM)
EXP2_SCALE = SCALE * math.log2(math.e)
BF = jnp.bfloat16
F32 = jnp.float32

ANY = pl.BlockSpec(memory_space=pl.ANY)
SMEM = pl.BlockSpec(memory_space=pltpu.SMEM)
VMEM = pl.BlockSpec(memory_space=pltpu.VMEM)
MB = 1024 * 1024


def shifted(block, axis, distance):
    size = lax.axis_size(axis)
    return lax.ppermute(block, axis, [(i, (i + distance) % size) for i in range(size)])


def to_sides(block):
    seqs, mps = lax.axis_size("seq"), lax.axis_size("mp")
    route = [
        (s * mps + m, s * mps + (m + (1 if s % 2 == 0 else -1)) % mps)
        for s in range(seqs)
        for m in range(mps)
    ]
    return lax.ppermute(block, ("seq", "mp"), route)


def core_swap(block):
    size = lax.axis_size("seq")
    return lax.ppermute(block, "seq", [(i, i ^ 1) for i in range(size)])


def turned(z):
    return (z + 1) % N_Z


def over_z(blocks):
    groups = [[2 * (n - 1) % (2 * N_Z) + core for n in range(N_Z)] for core in range(2)]
    return lax.all_to_all(blocks, "seq", 0, 0, axis_index_groups=groups, tiled=True)


def in_hbm(x):
    return pltpu.with_memory_space_constraint(x, pltpu.HBM)


def after(x, *others):
    def kernel(*refs):
        pass

    return pl.pallas_call(
        kernel,
        out_shape=sds(x.shape, x.dtype),
        in_specs=[ANY] * (1 + len(others)),
        out_specs=ANY,
        input_output_aliases={0: 0},
        compiler_params=params(1),
        cost_estimate=cost(0, 1024),
        name="after",
    )(x, *others)


def sds(shape, dtype=BF):
    return jax.ShapeDtypeStruct(shape, dtype)


def params(limit_mb):
    return pltpu.CompilerParams(vmem_limit_bytes=limit_mb * MB)


def cost(flops, nbytes, trans=0):
    return pl.CostEstimate(flops=flops, bytes_accessed=nbytes, transcendentals=trans)


def dot(a, b):
    return jnp.dot(a, b, preferred_element_type=F32)


def dot_t(a, b):
    return lax.dot_general(a, b, (((1,), (1,)), ((), ())), preferred_element_type=F32)


def run_copies(pairs, sems):
    copies = [pltpu.make_async_copy(s, d, sems.at[n]) for n, (s, d) in enumerate(pairs)]
    for c in copies:
        c.start()
    return copies


def fetch_kernel(idx0, idx1, idx2, idx3, memory, s0, s1, s2, s3, sems):
    me = lax.axis_index("enc")
    pairs = []
    for idx, out in ((idx0, s0), (idx1, s1), (idx2, s2), (idx3, s3)):
        for span in range(2):
            row = jnp.int32(0)
            for j in range(K_NB):
                flat = idx[span * K_NB + j]
                row = jnp.where(flat // DB == me, flat % DB, row)
            pairs.append((memory.at[row], out.at[pl.ds(span * NT, NT)]))
    for c in run_copies(pairs, sems):
        c.wait()


def fetch(idx, memory):
    cols = memory.shape[2]
    return pl.pallas_call(
        fetch_kernel,
        out_shape=[sds((2 * NT, cols))] * 4,
        in_specs=[SMEM] * 4 + [ANY],
        out_specs=[ANY] * 4,
        scratch_shapes=[pltpu.SemaphoreType.DMA((8,))],
        compiler_params=params(1),
        cost_estimate=cost(5 * 10**9, 1024),
        name="fetch",
    )(*idx, in_hbm(memory))


def compact_kernel(idx, r0, r1, r2, r3, out):
    me = lax.axis_index("enc")
    for span in range(2):
        for j in range(K_NB):
            at = (idx[span * K_NB + j] // DB - me + N_ENC) % N_ENC
            for k, r in enumerate((r0, r1, r2, r3)):

                @pl.when(at == k)
                def _():
                    begin = (span * K_NB + j) * NT
                    out[begin : begin + NT] = r[span * NT : (span + 1) * NT]


def compact(idx, received):
    rows, cols = received[0].shape
    return pl.pallas_call(
        compact_kernel,
        out_shape=sds((K_NB * rows, cols)),
        in_specs=[SMEM] + [VMEM] * 4,
        out_specs=VMEM,
        compiler_params=params(4),
        cost_estimate=cost(1 * 10**9, 1024),
        name="compact",
    )(idx, *received)


def source_columns(k, width):
    col = (lax.axis_index("mp") - k + N_MP) % N_MP
    return pl.ds(pl.multiple_of(col * width, width), width)


def attention(blocks):
    scores = [dot_t(q, k) for q, k, _ in blocks]
    tops = [jnp.max(s, axis=-1, keepdims=True) for s in scores]
    weights = [jnp.exp2((s - m) * EXP2_SCALE) for s, m in zip(scores, tops)]
    mixes = [dot(p.astype(BF), v) for p, (_, _, v) in zip(weights, blocks)]
    totals = [jnp.sum(p, axis=-1, keepdims=True) for p in weights]
    return [mix * (1.0 / total) for mix, total in zip(mixes, totals)]


def encode_kernel(x0, x1, x2, x3, wq, wk, wv, first, second, src_out, src, sems):
    width = x0.shape[1]
    pairs = [(x, src.at[:, source_columns(k, width)]) for k, x in enumerate((x0, x1, x2, x3))]
    for c in run_copies(pairs, sems):
        c.wait()
    kept = pltpu.make_async_copy(src, src_out, sems.at[0])
    kept.start()
    source = src[...]
    q, k, v = (dot(source, w[...]).astype(BF) for w in (wq, wk, wv))
    places = [
        (slice(n * NT, (n + 1) * NT), slice(h * HEAD_DIM, (h + 1) * HEAD_DIM))
        for n in range(src.shape[0] // NT)
        for h in range(width // HEAD_DIM)
    ]
    for at, mix in zip(places, attention([(q[at], k[at], v[at]) for at in places])):
        rows, cols = at
        out = (first, second)[rows.start // (K_NB * NT)]
        begin = rows.start % (K_NB * NT)
        out[begin : begin + NT, cols] = mix.astype(BF)
    kept.wait()


def encode(pieces, wq, wk, wv):
    rows, width = pieces[0].shape
    depth = wq.shape[0]
    return pl.pallas_call(
        encode_kernel,
        out_shape=[sds((rows // 2, width))] * 2 + [pltpu.HBM((rows, depth), BF)],
        in_specs=[ANY] * 4 + [VMEM] * 3,
        out_specs=[VMEM, VMEM, ANY],
        scratch_shapes=[pltpu.VMEM((rows, depth), BF), pltpu.SemaphoreType.DMA((4,))],
        compiler_params=params(12),
        cost_estimate=cost(30 * 10**9, 1024),
        name="encode",
    )(*pieces, wq, wk, wv)


def load_kernel(w0, w_near, w_half, s_near, s_half, heads, wq, wo_out, so, cq, sems):
    width = w0.shape[0]
    half = width // 2
    core = lax.axis_index("seq") % 2
    begins = [(w0, 0), (w_near, (1 + 2 * core) * width), (s_near, (3 - 2 * core) * width)]
    begins += [(w_half, 2 * width + core * half), (s_half, 2 * width + (1 - core) * half)]
    pairs = []
    for w, begin in begins:
        rows = w.shape[0]
        pairs.append((w, wo_out.at[pl.ds(pl.multiple_of(begin, half), rows)]))
    copies = run_copies(pairs, sems)
    for h in range(N_Z):
        cols = slice(h * HEAD_DIM, (h + 1) * HEAD_DIM)
        value = heads[turned(h)]
        so[:, cols] = value
        cq[:, cols] = dot(value, wq[h]).astype(BF)
    for c in copies:
        c.wait()


def load(wo, heads, wq):
    depth = wo[0].shape[1]
    tok, cols = heads.shape[1], N_Z * HEAD_DIM
    return pl.pallas_call(
        load_kernel,
        out_shape=[pltpu.VMEM((depth, depth), BF), sds((tok, cols)), sds((tok, cols))],
        in_specs=[ANY] * 5 + [VMEM] * 2,
        out_specs=[ANY, VMEM, VMEM],
        scratch_shapes=[pltpu.SemaphoreType.DMA((5,))],
        compiler_params=params(4),
        cost_estimate=cost(3 * 10**9, 1024),
        name="load",
    )(*map(in_hbm, wo[:3]), *wo[3:], heads, wq)


def cross_kernel(which, counts, src, a0, a1, a2, a3, wo, wk, wv, cq, so, out, src_s, attn, sems):
    nbrs, width = a0.shape
    pairs = [(a, attn.at[:, pl.ds(k * width, width)]) for k, a in enumerate((a0, a1, a2, a3))]
    copies = run_copies(pairs + [(src.at[pl.ds(which * nbrs, nbrs)], src_s)], sems)
    seq = lax.axis_index("seq")
    count = counts[0, seq * 2 + which]
    shape = (SPAN, nbrs)
    alive = lax.broadcasted_iota(jnp.int32, shape, 1) < count * NT
    if which == 1:
        past = (lax.broadcasted_iota(jnp.int32, shape, 0) > 0) & (seq == lax.axis_size("seq") - 1)
        alive = alive & jnp.logical_not(past)
    for c in copies[:4]:
        c.wait()
    mixed = dot(attn[...], wo[...])
    copies[4].wait()
    encoded = (src_s[...].astype(F32) + mixed).astype(BF)
    keys = dot(encoded, wk[...]).astype(BF)
    values = dot(encoded, wv[...]).astype(BF)
    rows = slice(which * SPAN, (which + 1) * SPAN)
    heads = [slice(h * HEAD_DIM, (h + 1) * HEAD_DIM) for h in range(cq.shape[1] // HEAD_DIM)]
    scores = [jnp.where(alive, dot_t(cq[rows, c], keys[:, c]), NEG_BIG) for c in heads]
    tops = [jnp.max(s, axis=-1, keepdims=True) for s in scores]
    weights = [jnp.exp2((s - m) * EXP2_SCALE) for s, m in zip(scores, tops)]
    weights = [jnp.where(alive, p, 0.0) for p in weights]
    mixes = [dot(p.astype(BF), values[:, c]) for p, c in zip(weights, heads)]
    totals = [jnp.sum(p, axis=-1, keepdims=True) for p in weights]
    for c, mix, total in zip(heads, mixes, totals):
        out[:, c] = (so[rows, c].astype(F32) + mix * (1.0 / jnp.maximum(total, 1.0))).astype(BF)


def cross(which, counts, source, attn, wo, wk, wv, cq, so):
    rows, depth = source.shape
    cols = cq.shape[1]

    def body(*refs):
        cross_kernel(which, *refs)

    return pl.pallas_call(
        body,
        out_shape=sds((SPAN, cols)),
        in_specs=[SMEM] + [ANY] * 5 + [VMEM] * 5,
        out_specs=VMEM,
        scratch_shapes=[
            pltpu.VMEM((rows // 2, depth), BF),
            pltpu.VMEM((rows // 2, depth), BF),
            pltpu.SemaphoreType.DMA((5,)),
        ],
        compiler_params=params(12),
        cost_estimate=cost(5 * 10**9, 1024),
        name="cross",
    )(counts, in_hbm(source), *attn, wo, wk, wv, cq, so)


def pack_kernel(q, k, v, wo, nbr_rows, nbr_owner, out, idx, half, rows, at_row, at_owner, sems):
    tok = q.shape[1]
    places = run_copies([(nbr_rows, at_row), (nbr_owner, at_owner)], sems)
    pairs = [(ref.at[0], rows.at[n]) for n, ref in enumerate((q, k, v))]
    count = half.shape[0]
    core = lax.axis_index("seq") % 2
    pairs.append((wo.at[pl.ds(pl.multiple_of(core * count, count), count)], half))
    copies = run_copies(pairs, sems.at[pl.ds(2, 4)])
    for c in places:
        c.wait()
    for span in range(2):
        for j in range(K_NB):
            idx[span * K_NB + j] = at_owner[0, span, j] * DB + at_row[0, span, j]
    for n, c in enumerate(copies[:3]):
        c.wait()
        for head in range(N_Z):
            cols = slice(head * HEAD_DIM, (head + 1) * HEAD_DIM)
            out[turned(head), n * tok : (n + 1) * tok, :] = rows[n, :, cols]
    copies[3].wait()


def pack(q, k, v, wo, nbr_rows, nbr_owner):
    _, tok, cols = q.shape
    return pl.pallas_call(
        pack_kernel,
        out_shape=[
            sds((N_Z, 3 * tok, HEAD_DIM)),
            sds((2 * K_NB,), jnp.int32),
            sds((wo.shape[0] // 2, wo.shape[1])),
        ],
        in_specs=[ANY] * 6,
        out_specs=[VMEM, SMEM, VMEM],
        scratch_shapes=[
            pltpu.VMEM((3, tok, cols), BF),
            pltpu.SMEM(nbr_rows.shape, jnp.int32),
            pltpu.SMEM(nbr_owner.shape, jnp.int32),
            pltpu.SemaphoreType.DMA((6,)),
        ],
        compiler_params=params(4),
        cost_estimate=cost(10**9, 1024),
        name="pack",
    )(*map(in_hbm, (q, k, v, wo, nbr_rows, nbr_owner)))


def attend_kernel(own, other, out):
    core = lax.axis_index("seq") % 2
    tok = out.shape[1]
    tokens = 2 * N_Z * tok

    def rows_of(ref, n, kind):
        at = slice(kind * tok, (kind + 1) * tok)
        rows = ref[1 : n + 1, at].reshape(-1, HEAD_DIM)
        return rows if n < N_Z else jnp.concatenate([rows, ref[0, at]], axis=0)

    def block_parts(z):
        here, after_z = turned(z), turned(turned(z))
        nxt = jnp.where(core == 0, other[here, :SPAN].astype(F32), other[after_z, :SPAN].astype(F32))
        both = jnp.concatenate([own[here, :tok].astype(F32), nxt], axis=0)
        rolled = pltpu.roll(both, both.shape[0] - (SPAN - 1), 0)[:tok].astype(BF)
        pos = (2 * z + core) * tok + SPAN - 1 + lax.broadcasted_iota(jnp.int32, (tok, 1), 0)
        pos = jnp.where(pos >= tokens, pos - tokens, pos)
        col = lax.broadcasted_iota(jnp.int32, (1, tok), 1)
        parts, values = [], []
        for n, ref, parity in ((z + 1, own, core), (min(z + 2, N_Z), other, 1 - core)):
            s = dot_t(rolled, rows_of(ref, n, 1))
            values.append(rows_of(ref, n, 2))
            for b in range(n):
                piece = s[:, b * tok : (b + 1) * tok]
                if b >= z or z == N_Z - 1:
                    piece = jnp.where((2 * b + parity) * tok + col <= pos, piece, NEG_BIG)
                parts.append(piece)
        return parts, values

    for group in ((0, 7, 3, 4), (1, 6, 2, 5)):
        made = [block_parts(z) for z in group]
        tops = [jnp.max(functools.reduce(jnp.maximum, parts), axis=-1, keepdims=True) for parts, _ in made]
        weights = [[jnp.exp2((s - m) * EXP2_SCALE) for s in parts] for (parts, _), m in zip(made, tops)]
        totals = [jnp.sum(functools.reduce(jnp.add, ps), axis=-1, keepdims=True) for ps in weights]
        mixes = []
        for ps, (_, (mine, theirs)) in zip(weights, made):
            p = jnp.concatenate([part.astype(BF) for part in ps], axis=1)
            split = mine.shape[0]
            mixes.append(dot(p[:, :split], mine) + dot(p[:, split:], theirs))
        for z, mix, total in zip(group, mixes, totals):
            out[turned(z)] = (mix * (1.0 / total)).astype(BF)


def attend(own, other):
    tok = own.shape[1] // 3
    total = N_Z * tok
    return pl.pallas_call(
        attend_kernel,
        out_shape=sds((N_Z, tok, HEAD_DIM)),
        in_specs=[VMEM] * 2,
        out_specs=VMEM,
        compiler_params=params(12),
        cost_estimate=cost(10 * 10**9, 1024),
        name="attend",
    )(own, other)


def place_kernel(received, first, second, out):
    rows = jnp.concatenate([received[...], first[...], second[...]], axis=0).astype(F32)
    out[0] = pltpu.roll(rows, rows.shape[0] - 1, 0)[: out.shape[1]].astype(BF)


def place(received, first, second):
    cols = first.shape[1]
    return pl.pallas_call(
        place_kernel,
        out_shape=sds((1, 2 * SPAN, cols)),
        in_specs=[VMEM] * 3,
        out_specs=VMEM,
        compiler_params=params(4),
        cost_estimate=cost(1 * 10**9, 1024),
        name="place",
    )(received, first, second)


def per_device(
    queries, keys_in, values_in, memory, enc_wq, enc_wk, enc_wv, enc_wo,
    cross_wk, cross_wv, cross_wq, nbr_rows, nbr_owner, nbr_count,
):
    packed, idx, wo_half = pack(queries, keys_in, values_in, enc_wo, nbr_rows, nbr_owner)
    packed = over_z(packed)
    asked = [idx] + [shifted(idx, "enc", k) for k in range(1, N_ENC)]
    near, far = to_sides(enc_wo), shifted(wo_half, "mp", 2)

    sent = fetch(asked, memory)
    received = [sent[0]] + [shifted(sent[k], "enc", -k) for k in range(1, N_ENC)]
    mine = compact(idx, received)
    pieces = [mine] + [shifted(mine, "mp", k) for k in range(1, N_MP)]

    packed = after(packed, mine, near, far)
    heads = over_z(attend(packed, core_swap(packed)))

    early, late, source = encode(pieces, enc_wq, enc_wk, enc_wv)
    late = [late] + [shifted(late, "mp", k) for k in range(1, N_MP)]
    wo, so, cq = load((enc_wo, near, far, core_swap(near), core_swap(far)), heads, cross_wq)
    early = after(early, wo)
    early = [early] + [shifted(early, "mp", k) for k in range(1, N_MP)]
    second = cross(1, nbr_count, source, late, wo, cross_wk, cross_wv, cq, so)
    passed = shifted(second, "seq", 1)
    first = cross(0, nbr_count, source, early, wo, cross_wk, cross_wv, cq, so)
    return place(passed, first, second)


def solution(mesh):
    return jax.shard_map(
        per_device,
        mesh=mesh,
        in_specs=(
            P("enc", "seq", "mp"),
            P("enc", "seq", "mp"),
            P("enc", "seq", "mp"),
            P("enc", None, "mp"),
            P(None, "mp"),
            P(None, "mp"),
            P(None, "mp"),
            P("mp", None),
            P(None, "mp"),
            P(None, "mp"),
            P("mp", None, None),
            P("enc", "seq", None),
            P("enc", "seq", None),
            P("enc", None),
        ),
        out_specs=P("enc", "seq", "mp"),
        check_vma=False,
    )
```
